128 devices in a mesh: dp: 64 (over z_hi, x, y, core), tensor: 2 (over z_lo).
Axes of the slice: x: 4, y: 4, z: 4 (z_hi: 2, z_lo: 2; z = z_hi * 2 + z_lo), core: 2. Of those that a mesh axis runs over, the one named last changes fastest.
Arguments:
- hidden_in: bfloat16 [128, 192, 1152], P('dp'), may hold values from -6 to 6
- row_layout: int32 [128, 4], P('dp'), may hold values from 1 to 96, 192 in all within a row
- cotangent: bfloat16 [128, 192, 1152], P('dp'), may hold values from -6 to 6
- pre_gain: float32 [1152], replicated, may hold values from 0.1 to 1.9
- pre_shift: float32 [1152], replicated, may hold values from -4 to 4
- query_weight: bfloat16 [1152, 1152], P(None, 'tensor'), may hold values from -0.25 to 0.25
- query_bias: float32 [1152], P('tensor'), may hold values from -6 to 6
- key_weight: bfloat16 [1152, 1152], P(None, 'tensor'), may hold values from -0.25 to 0.25
- value_weight: bfloat16 [1152, 1152], P(None, 'tensor'), may hold values from -0.1875 to 0.1875
- value_bias: float32 [1152], P('tensor'), may hold values from -6 to 6
- out_weight: bfloat16 [1152, 1152], P('tensor'), may hold values from -0.75 to 0.75
- out_bias: float32 [1152], replicated, may hold values from -4 to 4
- mid_gain: float32 [1152], replicated, may hold values from 0.1 to 1.9
- mid_shift: float32 [1152], replicated, may hold values from -4 to 4
- up_weight: bfloat16 [1152, 4304], P(None, 'tensor'), may hold values from -0.1875 to 0.1875
- up_bias: float32 [4304], P('tensor'), may hold values from -6 to 6
- down_weight: bfloat16 [4304, 1152], P('tensor'), may hold values from -0.09375 to 0.09375
- down_bias: float32 [1152], replicated, may hold values from -4 to 4
Outputs:
- mixed: bfloat16 [128, 192, 1152], P('dp')
- input_grad: bfloat16 [128, 192, 1152], P('dp')
- pre_gain_grad: float32 [1152], replicated
- pre_shift_grad: float32 [1152], replicated
- query_weight_grad: float32 [1152, 1152], P(None, 'tensor')
- query_bias_grad: float32 [1152], P('tensor')
- key_weight_grad: float32 [1152, 1152], P(None, 'tensor')
- value_weight_grad: float32 [1152, 1152], P(None, 'tensor')
- value_bias_grad: float32 [1152], P('tensor')
- out_weight_grad: float32 [1152, 1152], P('tensor')
- out_bias_grad: float32 [1152], replicated
- mid_gain_grad: float32 [1152], replicated
- mid_shift_grad: float32 [1152], replicated
- up_weight_grad: float32 [1152, 4304], P(None, 'tensor')
- up_bias_grad: float32 [4304], P('tensor')
- down_weight_grad: float32 [4304, 1152], P('tensor')
- down_bias_grad: float32 [1152], replicated
The draws below stay inside these ranges and needn't reach their ends.
Inputs may be any that keep to these rules, and one draw needn't show every extreme that they name: `row_layout`: each row's first 3 entries are its pictures' patch counts, the last entry the count of padding positions at the row's end; the entries of a row sum to 192, and the largest entry of each row is 96.
All inputs are finite; a program needn't handle non-finite values.
Results may differ from the reference program's by a relative error of at most 0.013.
The reference program's roundings to bfloat16 on the way count: a program that leaves them out, or rounds other values in their place, can miss the bound.
Values sent between devices are 32-bit elements; how exact they have to be, the bound alone decides.
No kernel may reach another device: no remote copies, remote signals or barrier semaphores. Data moves between devices by JAX's collectives and lax.ppermute only.
A program may use at most 192 MiB of HBM per device.

```python
import math
import jax
import jax.numpy as jnp
import numpy as np
from jax import lax

D = 1152
HEADS = 16
HEAD = 72
FF = 4304
ROW_LEN = 192
PICS = 3
PIC_MOST = 96
ROWS_DEV = 2
ROWS = 128


def level_of(key, dims, pieces, smallest, largest):
    def one(position, blocks):
        draws = jax.random.uniform(jax.random.fold_in(jax.random.fold_in(key, 6), position), (blocks,), jnp.float32, smallest / len(pieces), largest / len(pieces))
        return jnp.repeat(jnp.exp(draws), dims[position] // blocks).reshape((-1,) + (1,) * (len(dims) - position - 1))

    factor_of = one(*pieces[0])
    for cut in pieces[1:]:
        factor_of = factor_of * one(*cut)
    return factor_of


def split_up(count, total, most, slope):
    loads = [(1 << 20) // math.isqrt(grade ** slope) + 1 for grade in range(2, count + 1)]
    spare, given = total - most - (count - 1), [1] * (count - 1)
    while spare > 0:
        candidates = [i for i in range(count - 1) if given[i] < most]
        whole, budget = sum([loads[i] for i in candidates]), spare
        for i in candidates:
            extra = min(most - given[i], max(1, budget * loads[i] // whole), spare)
            given[i] = given[i] + extra
            spare = spare - extra
    return np.array([most] + given)


def uneven_parts(own_key, number_of, total, bound, skew):
    if number_of == 2:
        one = jax.random.randint(own_key, (), max(1, total - bound), min(bound, total - 1) + 1)
        return jnp.stack([one, total - one])
    tallies = jnp.asarray(split_up(number_of, total, bound, skew), jnp.int32)
    pairs = (number_of - 1) // 2
    giver, receiver = tallies[1:1 + 2 * pairs:2], tallies[2:2 + 2 * pairs:2]
    margin = jnp.minimum(giver - 1, bound - receiver)
    passed = jax.random.randint(jax.random.fold_in(own_key, 1), (pairs,), 0, 1 << 20) % (margin + 1)
    tallies = tallies.at[1:1 + 2 * pairs:2].set(giver - passed).at[2:2 + 2 * pairs:2].set(receiver + passed)
    return tallies[jax.random.permutation(jax.random.fold_in(own_key, 2), number_of)]


def noise(stream_key, dims, scale, reach, shards=(), held_as=jnp.bfloat16):
    values = scale * jax.random.normal(stream_key, dims, jnp.float32)
    if shards:
        values = values * level_of(stream_key, dims, shards, -0.22, 0.18)
    return jnp.clip(values, -reach, reach).astype(held_as)


def setup_inputs(seed: int = 0) -> dict:
    splits = jax.random.split(jax.random.key(seed), 19)
    return {
        "hidden_in": noise(splits[0], (ROWS, ROW_LEN, D), 1.0, 6.0, ((0, 64),)),
        "row_layout": jax.vmap(lambda own: uneven_parts(own, PICS + 1, ROW_LEN, PIC_MOST, 1))(jax.random.split(splits[1], ROWS)).reshape((ROWS, PICS + 1)).astype(jnp.int32),
        "cotangent": noise(splits[2], (ROWS, ROW_LEN, D), 1.0, 6.0, ((0, 64),)),
        "pre_gain": jnp.clip(1.0 + 0.18 * jax.random.normal(splits[3], (D,), jnp.float32), 0.1, 1.9),
        "pre_shift": noise(splits[4], (D,), 0.3, 4.0, (), jnp.float32),
        "query_weight": noise(splits[5], (D, D), (D // 2) ** -0.5, 0.25, ((1, 2),)),
        "query_bias": noise(splits[6], (D,), 0.5, 6.0, ((0, 2),), jnp.float32),
        "key_weight": noise(splits[7], (D, D), (D // 2) ** -0.5, 0.25, ((1, 2),)),
        "value_weight": noise(splits[8], (D, D), D ** -0.5, 0.1875, ((1, 2),)),
        "value_bias": noise(splits[9], (D,), 0.5, 6.0, ((0, 2),), jnp.float32),
        "out_weight": noise(splits[10], (D, D), (D // 16) ** -0.5, 0.75, ((0, 2),)),
        "out_bias": noise(splits[11], (D,), 0.3, 4.0, (), jnp.float32),
        "mid_gain": jnp.clip(1.0 + 0.18 * jax.random.normal(splits[12], (D,), jnp.float32), 0.1, 1.9),
        "mid_shift": noise(splits[13], (D,), 0.3, 4.0, (), jnp.float32),
        "up_weight": noise(splits[14], (D, FF), D ** -0.5, 0.1875, ((1, 2),)),
        "up_bias": noise(splits[15], (FF,), 0.5, 6.0, ((0, 2),), jnp.float32),
        "down_weight": noise(splits[16], (FF, D), FF ** -0.5, 0.09375, ((0, 2),)),
        "down_bias": noise(splits[17], (D,), 0.3, 4.0, (), jnp.float32),
    }


@jax.custom_vjp
def low(v):
    return lax.optimization_barrier(v.astype(jnp.bfloat16)).astype(jnp.float32)

@jax.custom_vjp
def low_back(v):
    return v

def low_keep(v):
    return (low(v), None)

def low_pass(kept, grad):
    return (grad,)

def back_keep(v):
    return (v, None)

def back_low(kept, grad):
    return (low(grad),)
low.defvjp(low_keep, low_pass)
low_back.defvjp(back_keep, back_low)
norm_epsilon = 1e-06

def layer_norm(values, norm_gain, norm_shift):
    center = values - lax.optimization_barrier(jnp.mean(values, axis=-1, keepdims=True))
    spread = lax.optimization_barrier(jnp.mean(center * center, axis=-1, keepdims=True))
    return center * lax.rsqrt(spread + norm_epsilon) * norm_gain + norm_shift

def matmul(left, right):
    return jnp.dot(left, right, precision=lax.Precision.HIGHEST)

def segments(layout, length):
    bounds = jnp.cumsum(layout[:, :-1], axis=1).astype(jnp.int32)
    places = jnp.arange(length, dtype=jnp.int32)
    inside = (places[None, :, None] >= bounds[:, None, :]).astype(jnp.int32)
    return lax.optimization_barrier(jnp.sum(inside, axis=2)).astype(jnp.int32)

def attend_row(inputs):
    queries, keys_row, values_row, segment_row = inputs
    scale_factor = HEAD ** (-0.5)
    scores = jnp.einsum('qhd,khd->hqk', queries, keys_row, precision=lax.Precision.HIGHEST) * scale_factor
    scores = low_back(scores)
    same_picture = segment_row[:, None] == segment_row[None, :]
    scores = jnp.where(same_picture[None], scores, -1000000000.0)
    probs = low(jax.nn.softmax(scores, axis=-1))
    return jnp.einsum('hqk,khd->qhd', probs, values_row, precision=lax.Precision.HIGHEST)

def layer(block_in, segment_block, weights):
    pre_gain, pre_shift, query_weight, query_bias, key_weight, value_weight, value_bias, out_weight, out_bias, mid_gain, mid_shift, up_weight, up_bias, down_weight, down_bias = weights
    row_count = block_in.shape[0]
    flat = block_in.reshape(row_count * ROW_LEN, D)
    normed = low(layer_norm(flat, pre_gain, pre_shift))
    queries = low_back(low(matmul(normed, query_weight) + query_bias))
    keys_all = low_back(low(matmul(normed, key_weight)))
    values_all = low_back(low(matmul(normed, value_weight) + value_bias))
    head_shape = (row_count, ROW_LEN, HEADS, HEAD)
    attended = lax.map(jax.checkpoint(attend_row), (queries.reshape(head_shape), keys_all.reshape(head_shape), values_all.reshape(head_shape), segment_block))
    attended = low_back(low(attended.reshape(row_count * ROW_LEN, D)))
    branch = low_back(matmul(attended, out_weight) + out_bias)
    resid = flat + branch
    middle = low(layer_norm(resid, mid_gain, mid_shift))
    pre_act = low_back(matmul(middle, up_weight) + up_bias)
    activ = low(jax.nn.gelu(pre_act, approximate=True))
    result = resid + matmul(activ, down_weight) + down_bias
    return result.reshape(row_count, ROW_LEN, D)

def reference(hidden_in, row_layout, cotangent, pre_gain, pre_shift, query_weight, query_bias, key_weight, value_weight, value_bias, out_weight, out_bias, mid_gain, mid_shift, up_weight, up_bias, down_weight, down_bias):
    params = tuple((member.astype(jnp.float32) for member in (pre_gain, pre_shift, query_weight, query_bias, key_weight, value_weight, value_bias, out_weight, out_bias, mid_gain, mid_shift, up_weight, up_bias, down_weight, down_bias)))
    groups = ROWS // ROWS_DEV
    inputs_grouped = hidden_in.reshape(groups, ROWS_DEV, ROW_LEN, D)
    layout_grouped = row_layout.reshape(groups, ROWS_DEV, PICS + 1)
    cot_grouped = cotangent.reshape(groups, ROWS_DEV, ROW_LEN, D)

    def group_step(totals, inputs):
        block_in, block_layout, block_cot = inputs
        segment_block = segments(block_layout, ROW_LEN)

        def forward(block_values, *weights):
            return layer(block_values, segment_block, weights)
        outputs, pullback = jax.vjp(forward, block_in.astype(jnp.float32), *params)
        grads = pullback(block_cot.astype(jnp.float32))
        new_totals = tuple((total + grad for total, grad in zip(totals, grads[1:])))
        return (new_totals, (outputs.astype(jnp.bfloat16), grads[0].astype(jnp.bfloat16)))
    start = tuple((jnp.zeros(member.shape, jnp.float32) for member in params))
    totals, (mixed, input_grad) = lax.scan(group_step, start, (inputs_grouped, layout_grouped, cot_grouped))
    mixed = mixed.reshape(ROWS, ROW_LEN, D)
    input_grad = input_grad.reshape(ROWS, ROW_LEN, D)
    return (mixed, input_grad, totals[0], totals[1], totals[2], totals[3], totals[4], totals[5], totals[6], totals[7], totals[8], totals[9], totals[10], totals[11], totals[12], totals[13], totals[14])
```

```python
import jax
import jax.numpy as jnp
from jax import lax
from jax.sharding import PartitionSpec as P

HEAD = 72
norm_epsilon = 1e-06


def partner_pairs(move):
    pairs = []
    for place in range(64):
        z_hi, x, y, core = place >> 5, (place >> 3) & 3, (place >> 1) & 3, place & 1
        z_hi, x, y, core = move(z_hi, x, y, core)
        pairs.append((place, ((z_hi * 4 + x) * 4 + y) * 2 + core))
    return pairs


PAIRS = {
    "core": partner_pairs(lambda z, x, y, c: (z, x, y, 1 - c)),
    "xa": partner_pairs(lambda z, x, y, c: (z, x ^ 1, y, c)),
    "xb": partner_pairs(lambda z, x, y, c: (z, x ^ 3, y, c)),
    "ya": partner_pairs(lambda z, x, y, c: (z, x, y ^ 1, c)),
    "yb": partner_pairs(lambda z, x, y, c: (z, x, y ^ 3, c)),
    "z": partner_pairs(lambda z, x, y, c: (1 - z, x, y, c)),
}
ORDERS = (
    ("xa", "ya", "xb", "yb"),
    ("ya", "xb", "yb", "xa"),
    ("xb", "yb", "xa", "ya"),
    ("yb", "xa", "ya", "xb"),
)


def sides():
    place = lax.axis_index("dp")
    x = (place >> 3) & 3
    y = (place >> 1) & 3
    return {
        "core": place & 1,
        "xa": (x ^ (x >> 1)) & 1,
        "xb": x >> 1,
        "ya": (y ^ (y >> 1)) & 1,
        "yb": y >> 1,
    }


def swap(values, pair):
    return lax.ppermute(values, "dp", PAIRS[pair])


def swap_tensor(values):
    return lax.ppermute(values, "tensor", [(0, 1), (1, 0)])


def half_of(values, side):
    count = values.shape[0] // 2
    return lax.dynamic_slice_in_dim(values, side * count, count, 0)


def scatter_step(values, pair, side):
    received = swap(half_of(values, 1 - side[pair]), pair)
    return half_of(values, side[pair]) + received


def joined(own, received, side):
    return jnp.where(
        side == 0,
        jnp.concatenate([own, received], 0),
        jnp.concatenate([received, own], 0),
    )


def gather_step(values, pair, side):
    return joined(values, swap(values, pair), side[pair])


def stream_sum(values, order, side):
    for pair in order[:3]:
        values = scatter_step(values, pair, side)
    values = values + swap(values, order[3])
    values = values + swap(values, "z")
    for pair in order[2::-1]:
        values = gather_step(values, pair, side)
    return values


def core_streams(send, keep, splits, first_order, side):
    rows, columns = keep.shape
    own = keep + swap(send, "core")
    parts = []
    begin = 0
    for number, block in enumerate(splits):
        part = own[begin : begin + 8 * block].reshape(8, block, columns)
        begin += 8 * block
        part = stream_sum(part, ORDERS[(first_order + number) % 4], side)
        parts.append(part.reshape(8 * block, columns))
    half = jnp.concatenate(parts, 0) if len(parts) > 1 else parts[0]
    return joined(half, swap(half, "core"), side["core"])


def normalized(values):
    center = values - jnp.mean(values, axis=-1, keepdims=True)
    spread = jnp.mean(center * center, axis=-1, keepdims=True)
    factor = lax.rsqrt(spread + norm_epsilon)
    return center * factor, factor


def norm_back(grad, normal, factor, gain):
    scaled = grad * gain
    mean_scaled = jnp.mean(scaled, axis=-1, keepdims=True)
    mean_normal = jnp.mean(scaled * normal, axis=-1, keepdims=True)
    return factor * (scaled - mean_scaled - normal * mean_normal)


def gelu_tanh(values):
    return jax.nn.gelu(values, approximate=True)


def product(left, right):
    return jnp.dot(left, right, preferred_element_type=jnp.float32)


def inner_rows(left, right):
    return lax.dot_general(
        left, right, (((0,), (0,)), ((), ())), preferred_element_type=jnp.float32
    )


def against(left, right):
    return lax.dot_general(
        left, right, (((1,), (1,)), ((), ())), preferred_element_type=jnp.float32
    )


def segments(layout, length):
    bounds = jnp.cumsum(layout[:, :-1], axis=1)
    places = jnp.arange(length, dtype=jnp.int32)
    inside = (places[None, :, None] >= bounds[:, None, :]).astype(jnp.int32)
    return jnp.sum(inside, axis=2)


def column_half(values, side):
    count = values.shape[1] // 2
    return jnp.where(side == 0, values[:, :count], values[:, count:])


def shards(
    hidden_in,
    row_layout,
    cotangent,
    pre_gain,
    pre_shift,
    query_weight,
    query_bias,
    key_weight,
    value_weight,
    value_bias,
    out_weight,
    out_bias,
    mid_gain,
    mid_shift,
    up_weight,
    up_bias,
    down_weight,
    down_bias,
):
    rows, length, width = hidden_in.shape
    tokens = rows * length
    heads_here = query_weight.shape[1] // HEAD
    hidden = up_weight.shape[1]
    scale_factor = HEAD ** (-0.5)
    head_shape = (rows, length, heads_here, HEAD)
    side = sides()
    core = side["core"]

    inputs = hidden_in.reshape(tokens, width).astype(jnp.float32)
    segment = segments(row_layout, length)
    same_picture = (segment[:, :, None] == segment[:, None, :])[:, None]
    pre_normal, pre_factor = normalized(inputs)
    normed = (pre_normal * pre_gain + pre_shift).astype(jnp.bfloat16)
    queries = (product(normed, query_weight) + query_bias).astype(jnp.bfloat16)
    keys = product(normed, key_weight).astype(jnp.bfloat16)
    values = (product(normed, value_weight) + value_bias).astype(jnp.bfloat16)
    queries = queries.reshape(head_shape)
    keys = keys.reshape(head_shape)
    values = values.reshape(head_shape)
    raw = jnp.einsum("bqhd,bkhd->bhqk", queries, keys, preferred_element_type=jnp.float32)
    scores = jnp.where(same_picture, raw * scale_factor, -1000000000.0)
    maximum = jnp.max(scores, axis=-1, keepdims=True)
    exponent = jnp.exp(scores - maximum)
    probs = exponent / jnp.sum(exponent, axis=-1, keepdims=True)
    probs_low = probs.astype(jnp.bfloat16)
    attended = jnp.einsum("bhqk,bkhd->bqhd", probs_low, values, preferred_element_type=jnp.float32)
    attended = attended.astype(jnp.bfloat16).reshape(tokens, heads_here * HEAD)
    branch = product(attended, out_weight)
    branch = branch + swap_tensor(branch)
    resid = inputs + (branch + out_bias)
    mid_normal, mid_factor = normalized(resid)
    middle = (mid_normal * mid_gain + mid_shift).astype(jnp.bfloat16)
    pre_act = product(middle, up_weight) + up_bias
    activ_float, gelu_pull = jax.vjp(gelu_tanh, pre_act)
    activ = activ_float.astype(jnp.bfloat16)

    cot_low = cotangent.reshape(tokens, width)
    cot_float = cot_low.astype(jnp.float32)
    down_bias_grad = jnp.sum(cot_float, axis=0)
    padded = -(-hidden // 128) * 128
    activ_wide = jnp.pad(activ, ((0, 0), (0, padded - hidden)))
    down_grad = core_streams(
        inner_rows(column_half(activ_wide, 1 - core), cot_low),
        inner_rows(column_half(activ_wide, core), cot_low),
        (72, 64),
        0,
        side,
    )[:hidden]
    act_grad = against(cot_low, down_weight)
    pre_grad = gelu_pull(act_grad)[0].astype(jnp.bfloat16)
    up_bias_grad = jnp.sum(pre_grad.astype(jnp.float32), axis=0)
    up_grad = core_streams(
        inner_rows(column_half(middle, 1 - core), pre_grad),
        inner_rows(column_half(middle, core), pre_grad),
        (40, 32),
        2,
        side,
    )
    mid_part = against(pre_grad, up_weight)
    mid_grad = mid_part + swap_tensor(mid_part)
    output_part = product(activ, down_weight)
    output = resid + (output_part + swap_tensor(output_part)) + down_bias
    mid_gain_grad = jnp.sum(mid_grad * mid_normal, axis=0)
    mid_shift_grad = jnp.sum(mid_grad, axis=0)
    resid_grad = cot_float + norm_back(mid_grad, mid_normal, mid_factor, mid_gain)

    branch_grad = resid_grad.astype(jnp.bfloat16)
    out_bias_grad = jnp.sum(branch_grad.astype(jnp.float32), axis=0)
    attended_wide = jnp.pad(attended, ((0, 0), (0, 640 - heads_here * HEAD)))
    out_grad = core_streams(
        inner_rows(column_half(attended_wide, 1 - core), branch_grad),
        inner_rows(column_half(attended_wide, core), branch_grad),
        (40,),
        3,
        side,
    )[: heads_here * HEAD]
    attended_grad = against(branch_grad, out_weight).astype(jnp.bfloat16).reshape(head_shape)
    value_grad = jnp.einsum(
        "bhqk,bqhd->bkhd", probs_low, attended_grad, preferred_element_type=jnp.float32
    ).astype(jnp.bfloat16)
    prob_grad = jnp.einsum(
        "bqhd,bkhd->bhqk", attended_grad, values, preferred_element_type=jnp.float32
    )
    score_grad = (
        probs * (prob_grad - jnp.sum(prob_grad * probs, axis=-1, keepdims=True))
    ).astype(jnp.bfloat16)
    query_grad = jnp.einsum("bhqk,bkhd->bqhd", score_grad, keys, preferred_element_type=jnp.float32)
    key_grad = jnp.einsum("bhqk,bqhd->bkhd", score_grad, queries, preferred_element_type=jnp.float32)
    query_grad = (query_grad * scale_factor).astype(jnp.bfloat16).reshape(tokens, -1)
    key_grad = (key_grad * scale_factor).astype(jnp.bfloat16).reshape(tokens, -1)
    value_grad = value_grad.reshape(tokens, -1)
    normed_send = column_half(normed, 1 - core)
    normed_keep = column_half(normed, core)
    weight_grads = [
        core_streams(
            inner_rows(normed_send, grad),
            inner_rows(normed_keep, grad),
            (72,),
            number,
            side,
        )
        for number, grad in enumerate((query_grad, key_grad, value_grad))
    ]
    query_bias_grad = jnp.sum(query_grad.astype(jnp.float32), axis=0)
    value_bias_grad = jnp.sum(value_grad.astype(jnp.float32), axis=0)
    normed_part = (
        against(query_grad, query_weight)
        + against(key_grad, key_weight)
        + against(value_grad, value_weight)
    )
    normed_grad = normed_part + swap_tensor(normed_part)
    pre_gain_grad = jnp.sum(normed_grad * pre_normal, axis=0)
    pre_shift_grad = jnp.sum(normed_grad, axis=0)
    input_grad = resid_grad + norm_back(normed_grad, pre_normal, pre_factor, pre_gain)

    small = jnp.concatenate(
        [
            pre_gain_grad,
            pre_shift_grad,
            out_bias_grad,
            mid_gain_grad,
            mid_shift_grad,
            down_bias_grad,
            query_bias_grad,
            value_bias_grad,
            up_bias_grad,
            jnp.zeros((2 * width - hidden,), jnp.float32),
        ]
    ).reshape(9, width)
    for pair in ("core", "xa", "ya", "xb", "yb", "z"):
        small = small + swap(small, pair)
    heads_wide = heads_here * HEAD
    return (
        output.astype(jnp.bfloat16).reshape(hidden_in.shape),
        input_grad.astype(jnp.bfloat16).reshape(hidden_in.shape),
        small[0],
        small[1],
        weight_grads[0],
        small[6, :heads_wide],
        weight_grads[1],
        weight_grads[2],
        small[6, heads_wide:],
        out_grad,
        small[2],
        small[3],
        small[4],
        up_grad,
        small[7:].reshape(-1)[:hidden],
        down_grad,
        small[5],
    )


def solution(mesh):
    placed = (
        P("dp", None, None),
        P("dp", None),
        P("dp", None, None),
        P(),
        P(),
        P(None, "tensor"),
        P("tensor"),
        P(None, "tensor"),
        P(None, "tensor"),
        P("tensor"),
        P("tensor", None),
        P(),
        P(),
        P(),
        P(None, "tensor"),
        P("tensor"),
        P("tensor", None),
        P(),
    )
    return jax.shard_map(
        shards,
        mesh=mesh,
        in_specs=placed,
        out_specs=(
            P("dp", None, None),
            P("dp", None, None),
            P(),
            P(),
            P(None, "tensor"),
            P("tensor"),
            P(None, "tensor"),
            P(None, "tensor"),
            P("tensor"),
            P("tensor", None),
            P(),
            P(),
            P(),
            P(None, "tensor"),
            P("tensor"),
            P("tensor", None),
            P(),
        ),
        check_vma=False,
    )
```

```python
import jax
import jax.numpy as jnp
from jax import lax
from jax.experimental import pallas as pl
from jax.experimental.pallas import tpu as pltpu
from jax.sharding import PartitionSpec as P

HEAD = 72
norm_epsilon = 1e-06


def partner_pairs(move):
    pairs = []
    for place in range(64):
        z_hi, x, y, core = place >> 5, (place >> 3) & 3, (place >> 1) & 3, place & 1
        z_hi, x, y, core = move(z_hi, x, y, core)
        pairs.append((place, ((z_hi * 4 + x) * 4 + y) * 2 + core))
    return pairs


PAIRS = {
    "core": partner_pairs(lambda z, x, y, c: (z, x, y, 1 - c)),
    "xa": partner_pairs(lambda z, x, y, c: (z, x ^ 1, y, c)),
    "xb": partner_pairs(lambda z, x, y, c: (z, x ^ 3, y, c)),
    "ya": partner_pairs(lambda z, x, y, c: (z, x, y ^ 1, c)),
    "yb": partner_pairs(lambda z, x, y, c: (z, x, y ^ 3, c)),
    "z": partner_pairs(lambda z, x, y, c: (1 - z, x, y, c)),
}
PLANES = [
    [((z_hi * 4 + x) * 4 + y) * 2 + core for x in range(4) for y in range(4)]
    for z_hi in range(2)
    for core in range(2)
]
ORDERS = (
    ("xa", "ya", "xb", "yb"),
    ("ya", "xb", "yb", "xa"),
    ("xb", "yb", "xa", "ya"),
    ("yb", "xa", "ya", "xb"),
)


def sides():
    place = lax.axis_index("dp")
    x = (place >> 3) & 3
    y = (place >> 1) & 3
    return {
        "core": place & 1,
        "xa": (x ^ (x >> 1)) & 1,
        "xb": x >> 1,
        "ya": (y ^ (y >> 1)) & 1,
        "yb": y >> 1,
    }


def swap(values, pair):
    return lax.ppermute(values, "dp", PAIRS[pair])


def swap_tensor(values):
    return lax.ppermute(values, "tensor", [(0, 1), (1, 0)])


class Cell:
    def __init__(self, value):
        self.value = value


class Order:
    def __init__(self):
        self.last = None

    def run(self, operation, ready):
        if self.last is not None:
            self.last.value, ready = lax.optimization_barrier((self.last.value, ready))
        self.last = Cell(operation(ready))
        return self.last


def half_of(values, side):
    count = values.shape[0] // 2
    return lax.dynamic_slice_in_dim(values, side * count, count, 0)


def row_half_of(values, side):
    count = values.shape[1] // 2
    return jnp.where(side == 0, values[:, :count], values[:, count:])


def joined(own, received, side, axis):
    return jnp.where(
        side == 0,
        jnp.concatenate([own, received], axis),
        jnp.concatenate([received, own], axis),
    )


class Stream:
    def __init__(self, name, order, pairs, side):
        self.name = name
        self.order = order
        self.pairs = pairs
        self.side = side
        self.stage = 0
        self.keep = None
        self.sent = None

    def begin(self, send, keep):
        four = (4, send.shape[0] // 4, send.shape[1])
        self.sent = Cell(send.reshape(four))
        self.order.last = self.sent
        self.keep = keep.reshape(four)
        self.stage = 1

    def step(self):
        pairs = self.pairs
        stage = self.stage
        self.stage += 1
        keep = self.keep
        with jax.named_scope(self.name + "_move_" + str(stage)):
            if stage <= 4:
                received = swap(self.sent.value, pairs[stage - 1])
            elif stage == 5:
                received = swap(self.sent.value, "z")
            else:
                pair = pairs[9 - stage]
                received = swap(self.sent.value, pair)
        with jax.named_scope(self.name + "_sum_" + str(stage)):
            if stage <= 3:
                take = half_of if stage < 3 else row_half_of
                side = self.side[pairs[stage]]
                self.keep = take(keep, side) + take(received, side)
                self.sent = self.order.run(
                    lambda ready: take(ready, 1 - side) + take(received, 1 - side), keep
                )
            elif stage == 4:
                self.sent = self.order.run(lambda ready: ready + received, keep)
            elif stage == 5:
                self.sent = self.order.run(lambda ready: ready + received, self.sent.value)
            else:
                axis = 1 if stage == 6 else 0
                self.sent = self.order.run(
                    lambda ready: joined(ready, received, self.side[pair], axis), self.sent.value
                )

    def pieces(self):
        whole = self.sent.value
        whole = whole.reshape(-1, whole.shape[2])
        with jax.named_scope(self.name + "_core"):
            return whole, swap(whole, "core")


def sent_gradient(left, right, parts):
    tokens, count = left.shape
    columns = right.shape[1]
    piece = count // (4 * parts)

    def kernel(left_ref, right_ref, *refs):
        turned_ref = refs[parts]
        step = pl.program_id(0)

        @pl.when(step == 0)
        def _():
            turned_ref[...] = left_ref[...].T

        rows = turned_ref[pl.ds(pl.multiple_of(step * piece, 16), piece), :]
        result = jnp.dot(rows, right_ref[...], preferred_element_type=jnp.float32)
        for part in range(parts):

            @pl.when(step // 4 == part)
            def _():
                refs[part][...] = result

    def place(part):
        return pl.BlockSpec(
            (piece, columns), lambda step: (jnp.clip(step - 4 * part, 0, 3), 0)
        )

    return pl.pallas_call(
        kernel,
        grid=(4 * parts,),
        in_specs=[
            pl.BlockSpec((tokens, count), lambda step: (0, 0)),
            pl.BlockSpec((tokens, columns), lambda step: (0, 0)),
        ],
        out_specs=[place(part) for part in range(parts)],
        out_shape=[jax.ShapeDtypeStruct((count // parts, columns), jnp.float32)] * parts,
        scratch_shapes=[pltpu.VMEM((count, tokens), jnp.bfloat16)],
        compiler_params=pltpu.CompilerParams(vmem_limit_bytes=40 * 1024 * 1024),
        cost_estimate=pl.CostEstimate(
            flops=2 * tokens * count * columns,
            bytes_accessed=4 * count * columns,
            transcendentals=0,
        ),
    )(left, right)


def whole_gradient(left, right, received):
    tokens, count = left.shape
    columns = right.shape[1]
    parts = len(received)
    piece = count // (4 * parts)

    def kernel(left_ref, right_ref, *refs):
        out_ref, turned_ref = refs[parts:]
        step = pl.program_id(0)

        @pl.when(step == 0)
        def _():
            turned_ref[...] = left_ref[...].T

        rows = turned_ref[pl.ds(pl.multiple_of(step * piece, 16), piece), :]
        result = jnp.dot(rows, right_ref[...], preferred_element_type=jnp.float32)
        for part in range(parts):

            @pl.when(step // 4 == part)
            def _():
                out_ref[...] = result + refs[part][...]

    def place(part):
        return pl.BlockSpec(
            (piece, columns), lambda step: (jnp.clip(step - 4 * part, 0, 3), 0)
        )

    return pl.pallas_call(
        kernel,
        grid=(4 * parts,),
        in_specs=[
            pl.BlockSpec((tokens, count), lambda step: (0, 0)),
            pl.BlockSpec((tokens, columns), lambda step: (0, 0)),
        ]
        + [place(part) for part in range(parts)],
        out_specs=pl.BlockSpec((piece, columns), lambda step: (step, 0)),
        out_shape=jax.ShapeDtypeStruct((count, columns), jnp.float32),
        scratch_shapes=[pltpu.VMEM((count, tokens), jnp.bfloat16)],
        compiler_params=pltpu.CompilerParams(vmem_limit_bytes=48 * 1024 * 1024),
        cost_estimate=pl.CostEstimate(
            flops=2 * tokens * count * columns,
            bytes_accessed=8 * count * columns,
            transcendentals=0,
        ),
    )(left, right, *received)


def own_gradient(left, right, received, side, first, count):
    tokens, wide = left.shape
    columns = right.shape[1]
    piece = count // 4

    def place(step, here):
        return jnp.where(step < 2, (1 - here) * 2 + step, here * 2 + step - 2)

    def kernel(side_ref, left_ref, right_ref, received_ref, send_ref, keep_ref, turned_ref):
        step = pl.program_id(0)

        @pl.when(step == 0)
        def _():
            turned_ref[...] = left_ref[...].T

        begin = pl.multiple_of(first + place(step, side_ref[0]) * piece, 16)
        rows = turned_ref[pl.ds(begin, piece), :]
        total = jnp.dot(rows, right_ref[...], preferred_element_type=jnp.float32)
        total = total + received_ref[...]

        @pl.when(step < 2)
        def _():
            send_ref[...] = total

        @pl.when(step >= 2)
        def _():
            keep_ref[...] = total

    half = jax.ShapeDtypeStruct((count // 2, columns), jnp.float32)
    return pl.pallas_call(
        kernel,
        grid_spec=pltpu.PrefetchScalarGridSpec(
            num_scalar_prefetch=1,
            grid=(4,),
            in_specs=[
                pl.BlockSpec((tokens, wide), lambda step, here: (0, 0)),
                pl.BlockSpec((tokens, columns), lambda step, here: (0, 0)),
                pl.BlockSpec(
                    (piece, columns),
                    lambda step, here: (first // piece + place(step, here[0]), 0),
                ),
            ],
            out_specs=(
                pl.BlockSpec((piece, columns), lambda step, here: (jnp.minimum(step, 1), 0)),
                pl.BlockSpec((piece, columns), lambda step, here: (jnp.maximum(step - 2, 0), 0)),
            ),
            scratch_shapes=[pltpu.VMEM((wide, tokens), jnp.bfloat16)],
        ),
        out_shape=(half, half),
        compiler_params=pltpu.CompilerParams(vmem_limit_bytes=32 * 1024 * 1024),
        cost_estimate=pl.CostEstimate(
            flops=2 * tokens * count * columns,
            bytes_accessed=8 * count * columns,
            transcendentals=0,
        ),
    )(side.reshape(1), left, right, received)


def pick_rows(core, pieces, rows, block):
    columns = pieces[0][0].shape[1]
    counts = [own.shape[0] // block for own, _ in pieces]
    firsts = [sum(counts[:number]) for number in range(len(counts))]

    def kernel(core_ref, *refs):
        first_ref, second_ref = refs[-2:]
        here = pl.program_id(0)
        for number, (first, count) in enumerate(zip(firsts, counts)):
            own_ref, other_ref = refs[2 * number : 2 * number + 2]
            inside = (here >= first) & (here < first + count)

            @pl.when(inside & (core_ref[0] == 0))
            def _():
                first_ref[...] = own_ref[...]
                second_ref[...] = other_ref[...]

            @pl.when(inside & (core_ref[0] != 0))
            def _():
                first_ref[...] = other_ref[...]
                second_ref[...] = own_ref[...]

    def place(first, count):
        return pl.BlockSpec(
            (block, columns), lambda i, core_ref: (jnp.clip(i - first, 0, count - 1), 0)
        )

    specs = [place(first, count) for first, count in zip(firsts, counts) for _ in range(2)]
    shape = jax.ShapeDtypeStruct((rows, columns), jnp.float32)
    out_spec = pl.BlockSpec((block, columns), lambda i, core_ref: (i, 0))
    return pl.pallas_call(
        kernel,
        grid_spec=pltpu.PrefetchScalarGridSpec(
            num_scalar_prefetch=1,
            grid=(sum(counts),),
            in_specs=specs,
            out_specs=(out_spec, out_spec),
        ),
        out_shape=(shape, shape),
        compiler_params=pltpu.CompilerParams(vmem_limit_bytes=40 * 1024 * 1024),
        cost_estimate=pl.CostEstimate(
            flops=0, bytes_accessed=16 * rows * columns, transcendentals=0
        ),
    )(core.reshape(1), *[part for pair in pieces for part in pair])


def normalized(values):
    center = values - jnp.mean(values, axis=-1, keepdims=True)
    spread = jnp.mean(center * center, axis=-1, keepdims=True)
    factor = lax.rsqrt(spread + norm_epsilon)
    return center * factor, factor


def norm_back(grad, normal, factor, gain):
    scaled = grad * gain
    mean_scaled = jnp.mean(scaled, axis=-1, keepdims=True)
    mean_normal = jnp.mean(scaled * normal, axis=-1, keepdims=True)
    return factor * (scaled - mean_scaled - normal * mean_normal)


def gelu_tanh(values):
    return jax.nn.gelu(values, approximate=True)


def product(left, right):
    return jnp.dot(left, right, preferred_element_type=jnp.float32)


def inner_rows(left, right):
    return lax.dot_general(
        left, right, (((0,), (0,)), ((), ())), preferred_element_type=jnp.float32
    )


def against(left, right):
    return lax.dot_general(
        left, right, (((1,), (1,)), ((), ())), preferred_element_type=jnp.float32
    )


def segments(layout, length):
    bounds = jnp.cumsum(layout[:, :-1], axis=1)
    places = jnp.arange(length, dtype=jnp.int32)
    inside = (places[None, :, None] >= bounds[:, None, :]).astype(jnp.int32)
    return jnp.sum(inside, axis=2)


def shards(
    hidden_in,
    row_layout,
    cotangent,
    pre_gain,
    pre_shift,
    query_weight,
    query_bias,
    key_weight,
    value_weight,
    value_bias,
    out_weight,
    out_bias,
    mid_gain,
    mid_shift,
    up_weight,
    up_bias,
    down_weight,
    down_bias,
):
    rows, length, width = hidden_in.shape
    tokens = rows * length
    heads_wide = query_weight.shape[1]
    heads_here = heads_wide // HEAD
    hidden = up_weight.shape[1]
    padded = -(-hidden // 128) * 128
    scale_factor = HEAD ** (-0.5)
    head_shape = (length, heads_here, HEAD)
    side = sides()
    core = side["core"]
    order = Order()

    def row_of(values, row):
        return values[row * length : (row + 1) * length]

    inputs = hidden_in.reshape(tokens, width).astype(jnp.float32)
    segment = segments(row_layout, length)
    same_picture = (segment[:, :, None] == segment[:, None, :])[:, None]
    pre_normal, pre_factor = normalized(inputs)
    normed = (pre_normal * pre_gain + pre_shift).astype(jnp.bfloat16)
    queries = (product(normed, query_weight) + query_bias).astype(jnp.bfloat16)
    keys = product(normed, key_weight).astype(jnp.bfloat16)
    values = (product(normed, value_weight) + value_bias).astype(jnp.bfloat16)
    cot_low = cotangent.reshape(tokens, width)
    cot_float = cot_low.astype(jnp.float32)

    heads = []
    probs = []
    attended = []
    branch = []
    for row in range(rows):
        q, k, v = (row_of(part, row).reshape(head_shape) for part in (queries, keys, values))
        heads.append((q, k, v))
        raw = jnp.einsum("qhd,khd->hqk", q, k, preferred_element_type=jnp.float32)
        scores = jnp.where(same_picture[row], raw * scale_factor, -1000000000.0)
        maximum = jnp.max(scores, axis=-1, keepdims=True)
        exponent = jnp.exp(scores - maximum)
        probs.append(exponent / jnp.sum(exponent, axis=-1, keepdims=True))
        mixed = jnp.einsum(
            "hqk,khd->qhd",
            probs[row].astype(jnp.bfloat16),
            v,
            preferred_element_type=jnp.float32,
        )
        attended.append(mixed.astype(jnp.bfloat16).reshape(length, heads_wide))
        branch.append(order.run(lambda ready: product(ready, out_weight), attended[row]))
    act_grad = order.run(lambda ready: against(ready, down_weight), cot_low)

    resid = []
    mid_normal = []
    mid_factor = []
    middle = []
    activ = []
    pre_grad = []
    mid_part = []
    for row in range(rows):
        with jax.named_scope("branch_move_" + str(row)):
            received = swap_tensor(branch[row].value)
        resid.append(
            order.run(
                lambda ready: row_of(inputs, row) + ((ready + received) + out_bias),
                branch[row].value,
            )
        )
        normal, factor = normalized(resid[row].value)
        mid_normal.append(normal)
        mid_factor.append(factor)
        middle.append((normal * mid_gain + mid_shift).astype(jnp.bfloat16))
        pre_act = product(middle[row], up_weight) + up_bias
        activ_float, gelu_pull = jax.vjp(gelu_tanh, pre_act)
        activ.append(activ_float.astype(jnp.bfloat16))
        pre_grad.append(gelu_pull(row_of(act_grad.value, row))[0].astype(jnp.bfloat16))
        mid_part.append(order.run(lambda ready: against(ready, up_weight), pre_grad[row]))

    is_first = core == 0
    activ_all = jnp.concatenate(activ, 0)
    pre_grad_all = jnp.concatenate(pre_grad, 0)
    middle_all = jnp.concatenate(middle, 0)
    keep_right = jnp.where(is_first, cot_low, middle_all)
    send_right = jnp.where(is_first, middle_all, cot_low)
    widen = ((0, 0), (0, padded - hidden))
    m_send_left = jnp.pad(jnp.where(is_first, pre_grad_all, activ_all), widen)
    m_keep_left = jnp.pad(jnp.where(is_first, activ_all, pre_grad_all), widen)
    m_sends = order.run(lambda ready: sent_gradient(ready, send_right, 2), m_send_left)

    resid_grad = []
    branch_grad = []
    gain_terms = []
    row_grads = []

    def mid_back(row):
        with jax.named_scope("mid_move_" + str(row)):
            received = swap_tensor(mid_part[row].value)
        mid_grad = order.run(lambda ready: ready + received, mid_part[row].value).value
        gain_terms.append(
            (jnp.sum(mid_grad * mid_normal[row], axis=0), jnp.sum(mid_grad, axis=0))
        )
        resid_grad.append(
            row_of(cot_float, row) + norm_back(mid_grad, mid_normal[row], mid_factor[row], mid_gain)
        )
        branch_grad.append(resid_grad[row].astype(jnp.bfloat16))

    def attention_back(row, meanwhile):
        attended_grad = order.run(
            lambda ready: against(ready, out_weight).astype(jnp.bfloat16), branch_grad[row]
        )
        attended_grad = attended_grad.value.reshape(head_shape)
        q, k, v = heads[row]
        prob_grad = jnp.einsum("qhd,khd->hqk", attended_grad, v, preferred_element_type=jnp.float32)
        score_grad = order.run(
            lambda ready: (
                ready * (prob_grad - jnp.sum(prob_grad * ready, axis=-1, keepdims=True))
            ).astype(jnp.bfloat16),
            probs[row],
        )
        meanwhile()
        value_grad = jnp.einsum(
            "hqk,qhd->khd",
            probs[row].astype(jnp.bfloat16),
            attended_grad,
            preferred_element_type=jnp.float32,
        )
        query_grad = jnp.einsum(
            "hqk,khd->qhd", score_grad.value, k, preferred_element_type=jnp.float32
        )
        key_grad = jnp.einsum(
            "hqk,qhd->khd", score_grad.value, q, preferred_element_type=jnp.float32
        )
        row_grads.append(
            tuple(
                part.astype(jnp.bfloat16).reshape(length, heads_wide)
                for part in (query_grad * scale_factor, key_grad * scale_factor, value_grad)
            )
        )

    output_part = order.run(lambda ready: product(ready, down_weight), activ_all)
    m_received = []
    for number, part in enumerate(m_sends.value):
        with jax.named_scope("ff_core_move_" + str(number)):
            m_received.append(swap(part, "core"))
    m_own = order.run(lambda ready: whole_gradient(ready, keep_right, m_received), m_keep_left)
    with jax.named_scope("ff_scatter"):
        m_block = lax.psum_scatter(
            m_own.value, "dp", axis_index_groups=PLANES, scatter_dimension=0, tiled=True
        )
    mid_back(0)
    attention_back(0, lambda: None)
    mid_back(1)
    attention_back(1, lambda: None)
    mid_gain_grad = gain_terms[0][0] + gain_terms[1][0]
    mid_shift_grad = gain_terms[0][1] + gain_terms[1][1]

    query_grad, key_grad, value_grad = (
        jnp.concatenate([row_grads[row][place] for row in range(rows)], 0) for place in range(3)
    )
    attended_all = jnp.concatenate(attended, 0)
    branch_grad_all = jnp.concatenate(branch_grad, 0)
    n_streams = [Stream("at" + str(n), order, ORDERS[n], side) for n in (2, 3, 0, 1)]
    n_keep = (
        (jnp.where(is_first, query_grad, value_grad), normed),
        (
            jnp.where(is_first, key_grad, attended_all),
            jnp.where(is_first, normed, branch_grad_all),
        ),
    )
    n_send = (
        (jnp.where(is_first, value_grad, query_grad), normed),
        (
            jnp.where(is_first, attended_all, key_grad),
            jnp.where(is_first, branch_grad_all, normed),
        ),
    )
    with jax.named_scope("output_move"):
        received = swap_tensor(output_part.value)
    output = order.run(
        lambda ready: (
            jnp.concatenate([part.value for part in resid], 0) + (ready + received) + down_bias
        ).astype(jnp.bfloat16),
        output_part.value,
    )
    n_sends = []
    for left, right in n_send:
        n_sends.append(order.run(lambda ready: sent_gradient(ready, right, 1)[0], left))
    for n in range(2):
        left, right = n_keep[n]
        with jax.named_scope("at" + str(n) + "_core_move"):
            received = swap(n_sends[n].value, "core")
        for stream, first, count in (
            (n_streams[2 * n], 0, 320),
            (n_streams[2 * n + 1], 320, 256),
        ):
            here = side[stream.pairs[0]]
            halves = order.run(
                lambda ready: own_gradient(left, ready, received, here, first, count), right
            )
            stream.begin(*halves.value)
    normed_part = order.run(
        lambda ready: against(ready, query_weight)
        + against(key_grad, key_weight)
        + against(value_grad, value_weight),
        query_grad,
    )

    def n_step():
        for stream in n_streams:
            stream.step()

    n_step()
    m_block = order.run(lambda ready: ready + 0.0, m_block)
    with jax.named_scope("ff_z_move"):
        received = swap(m_block.value, "z")
    m_block = order.run(lambda ready: ready + received, m_block.value)
    with jax.named_scope("ff_gather"):
        m_whole = lax.all_gather(
            m_block.value, "dp", axis_index_groups=PLANES, axis=0, tiled=True
        )
    n_step()
    n_step()
    n_step()
    with jax.named_scope("normed_move"):
        received = swap_tensor(normed_part.value)
    normed_grad = order.run(lambda ready: ready + received, normed_part.value)
    pre_gain_grad = jnp.sum(normed_grad.value * pre_normal, axis=0)
    pre_shift_grad = jnp.sum(normed_grad.value, axis=0)
    input_grad = jnp.concatenate(resid_grad, 0) + norm_back(
        normed_grad.value, pre_normal, pre_factor, pre_gain
    )
    small = jnp.concatenate(
        [
            pre_gain_grad,
            pre_shift_grad,
            jnp.sum(branch_grad_all.astype(jnp.float32), axis=0),
            mid_gain_grad,
            mid_shift_grad,
            jnp.sum(cot_float, axis=0),
            jnp.sum(query_grad.astype(jnp.float32), axis=0),
            jnp.sum(value_grad.astype(jnp.float32), axis=0),
            jnp.sum(pre_grad_all.astype(jnp.float32), axis=0),
            jnp.zeros((2 * width - hidden,), jnp.float32),
        ]
    ).reshape(9, width)
    small = order.run(lambda ready: ready, small)

    def small_step(small, pair):
        with jax.named_scope("small_move_" + pair):
            received = swap(small.value, pair)
        return order.run(lambda ready: ready + received, small.value)

    small = small_step(small, "core")
    n_step()
    small = small_step(small, "z")
    n_step()
    m_whole = order.run(lambda ready: ready, m_whole)
    small = small_step(small, "xa")
    with jax.named_scope("ff_core_back"):
        received = swap(m_whole.value, "core")
    small = small_step(small, "ya")
    n_step()
    small = small_step(small, "xb")
    small = small_step(small, "yb")
    n_step()
    small = small.value
    picked = order.run(
        lambda ready: pick_rows(core, [(ready, received)], hidden, 128), m_whole.value
    )
    n_step()
    down_grad, up_grad = picked.value
    pieces = [stream.pieces() for stream in n_streams]
    query_weight_grad, value_weight_grad = pick_rows(core, pieces[:2], heads_wide, 64)
    key_weight_grad, out_grad = pick_rows(core, pieces[2:], heads_wide, 64)
    return (
        output.value.reshape(hidden_in.shape),
        input_grad.astype(jnp.bfloat16).reshape(hidden_in.shape),
        small[0],
        small[1],
        query_weight_grad.T,
        small[6, :heads_wide],
        key_weight_grad.T,
        value_weight_grad.T,
        small[6, heads_wide:],
        out_grad,
        small[2],
        small[3],
        small[4],
        up_grad.T,
        small[7:].reshape(-1)[:hidden],
        down_grad,
        small[5],
    )


def solution(mesh):
    placed = (
        P("dp", None, None),
        P("dp", None),
        P("dp", None, None),
        P(),
        P(),
        P(None, "tensor"),
        P("tensor"),
        P(None, "tensor"),
        P(None, "tensor"),
        P("tensor"),
        P("tensor", None),
        P(),
        P(),
        P(),
        P(None, "tensor"),
        P("tensor"),
        P("tensor", None),
        P(),
    )
    return jax.shard_map(
        shards,
        mesh=mesh,
        in_specs=placed,
        out_specs=(
            P("dp", None, None),
            P("dp", None, None),
            P(),
            P(),
            P(None, "tensor"),
            P("tensor"),
            P(None, "tensor"),
            P(None, "tensor"),
            P("tensor"),
            P("tensor", None),
            P(),
            P(),
            P(),
            P(None, "tensor"),
            P("tensor"),
            P("tensor", None),
            P(),
        ),
        check_vma=False,
    )
```

```python
import jax
import jax.numpy as jnp
from jax import lax
from jax.experimental import pallas as pl
from jax.experimental.pallas import tpu as pltpu
from jax.sharding import PartitionSpec as P

HEAD = 72
norm_epsilon = 1e-06


def partner_pairs(move):
    pairs = []
    for place in range(64):
        z_hi, x, y, core = place >> 5, (place >> 3) & 3, (place >> 1) & 3, place & 1
        z_hi, x, y, core = move(z_hi, x, y, core)
        pairs.append((place, ((z_hi * 4 + x) * 4 + y) * 2 + core))
    return pairs


PAIRS = {
    "core": partner_pairs(lambda z, x, y, c: (z, x, y, 1 - c)),
    "xa": partner_pairs(lambda z, x, y, c: (z, x ^ 1, y, c)),
    "xb": partner_pairs(lambda z, x, y, c: (z, x ^ 3, y, c)),
    "ya": partner_pairs(lambda z, x, y, c: (z, x, y ^ 1, c)),
    "yb": partner_pairs(lambda z, x, y, c: (z, x, y ^ 3, c)),
    "z": partner_pairs(lambda z, x, y, c: (1 - z, x, y, c)),
}
PLANES = [
    [((z_hi * 4 + x) * 4 + y) * 2 + core for x in range(4) for y in range(4)]
    for z_hi in range(2)
    for core in range(2)
]
ORDERS = (
    ("xa", "ya", "xb", "yb"),
    ("ya", "xb", "yb", "xa"),
    ("xb", "yb", "xa", "ya"),
    ("yb", "xa", "ya", "xb"),
)


def sides():
    place = lax.axis_index("dp")
    x = (place >> 3) & 3
    y = (place >> 1) & 3
    return {
        "core": place & 1,
        "xa": (x ^ (x >> 1)) & 1,
        "xb": x >> 1,
        "ya": (y ^ (y >> 1)) & 1,
        "yb": y >> 1,
    }


def swap(values, pair):
    return lax.ppermute(values, "dp", PAIRS[pair])


def swap_tensor(values):
    return lax.ppermute(values, "tensor", [(0, 1), (1, 0)])


class Cell:
    def __init__(self, value):
        self.value = value


class Order:
    def __init__(self):
        self.last = None

    def run(self, operation, ready):
        if self.last is not None:
            self.last.value, ready = lax.optimization_barrier((self.last.value, ready))
        self.last = Cell(operation(ready))
        return self.last

    def settle(self, value):
        self.last.value, value = lax.optimization_barrier((self.last.value, value))
        return value


def half_of(values, side):
    count = values.shape[0] // 2
    return lax.dynamic_slice_in_dim(values, side * count, count, 0)


def row_half_of(values, side):
    count = values.shape[1] // 2
    return jnp.where(side == 0, values[:, :count], values[:, count:])


def joined(own, received, side, axis):
    return jnp.where(
        side == 0,
        jnp.concatenate([own, received], axis),
        jnp.concatenate([received, own], axis),
    )


class Stream:
    def __init__(self, name, order, pairs, side):
        self.name = name
        self.order = order
        self.pairs = pairs
        self.side = side
        self.stage = 0
        self.keep = None
        self.sent = None

    def begin(self, send, keep):
        four = (4, send.shape[0] // 4, send.shape[1])
        self.sent = Cell(send.reshape(four))
        self.order.last = self.sent
        self.keep = keep.reshape(four)
        self.stage = 1

    def moved(self):
        pairs = self.pairs
        stage = self.stage
        with jax.named_scope(self.name + "_move_" + str(stage)):
            if stage <= 4:
                return swap(self.sent.value, pairs[stage - 1])
            if stage == 5:
                return swap(self.sent.value, "z")
            return swap(self.sent.value, pairs[9 - stage])

    def step(self, received):
        pairs = self.pairs
        stage = self.stage
        self.stage += 1
        keep = self.keep
        with jax.named_scope(self.name + "_sum_" + str(stage)):
            if stage <= 3:
                take = half_of if stage < 3 else row_half_of
                side = self.side[pairs[stage]]
                self.keep = take(keep, side) + take(received, side)
                self.sent = self.order.run(
                    lambda ready: take(ready, 1 - side) + take(received, 1 - side), keep
                )
            elif stage == 4:
                self.sent = self.order.run(lambda ready: ready + received, keep)
            elif stage == 5:
                self.sent = self.order.run(lambda ready: ready + received, self.sent.value)
            else:
                axis = 1 if stage == 6 else 0
                pair = pairs[9 - stage]
                self.sent = self.order.run(
                    lambda ready: joined(ready, received, self.side[pair], axis), self.sent.value
                )

    def halves(self):
        here = self.sent.value
        flat = (-1, here.shape[2])
        return here.reshape(flat), self.moved().reshape(flat)


def pick_rows(core, own, other, rows, block, skipped, first, total, kept=()):
    columns = own.shape[1]
    before, start = skipped // block, first // block

    def kernel(core_ref, own_ref, other_ref, *refs):
        first_ref, second_ref = refs[-2:]

        @pl.when(core_ref[0] == 0)
        def _():
            first_ref[...] = own_ref[...]
            second_ref[...] = other_ref[...]

        @pl.when(core_ref[0] != 0)
        def _():
            first_ref[...] = other_ref[...]
            second_ref[...] = own_ref[...]

    shape = jax.ShapeDtypeStruct((total, columns), jnp.float32)
    in_spec = pl.BlockSpec((block, columns), lambda i, core_ref: (before + i, 0))
    out_spec = pl.BlockSpec((block, columns), lambda i, core_ref: (start + i, 0))
    return pl.pallas_call(
        kernel,
        grid_spec=pltpu.PrefetchScalarGridSpec(
            num_scalar_prefetch=1,
            grid=(-(-rows // block),),
            in_specs=[in_spec, in_spec] + [pl.BlockSpec(memory_space=pl.ANY)] * len(kept),
            out_specs=(out_spec, out_spec),
        ),
        out_shape=(shape, shape),
        input_output_aliases={3 + number: number for number in range(len(kept))},
        compiler_params=limit(20),
        cost_estimate=estimate(0.02),
    )(core.reshape(1), own, other, *kept)


def pick_halves(core, sides, pieces, rows, first, before):
    half, columns = pieces[0].shape
    block = half // 2
    start = first // block

    def kernel(core_ref, sides_ref, *refs):
        first_ref, second_ref = refs[-2:]
        here = (pl.program_id(0) // 2) == sides_ref[0]
        for other in range(2):
            own_ref, far_ref = refs[other], refs[2 + other]
            chosen = here if other == 0 else jnp.logical_not(here)

            @pl.when(chosen & (core_ref[0] == 0))
            def _():
                first_ref[...] = own_ref[...]
                second_ref[...] = far_ref[...]

            @pl.when(chosen & (core_ref[0] != 0))
            def _():
                first_ref[...] = far_ref[...]
                second_ref[...] = own_ref[...]

    def place(other):
        def index(i, core_ref, sides_ref):
            side = sides_ref[0] if other == 0 else 1 - sides_ref[0]
            return (jnp.clip(i - side * 2, 0, 1), 0)

        return pl.BlockSpec((block, columns), index)

    shape = jax.ShapeDtypeStruct((rows, columns), jnp.float32)
    out_spec = pl.BlockSpec((block, columns), lambda i, core_ref, sides_ref: (start + i, 0))
    steps = min(4, -(-(rows - first) // block))
    kept = [] if before is None else list(before)
    return pl.pallas_call(
        kernel,
        grid_spec=pltpu.PrefetchScalarGridSpec(
            num_scalar_prefetch=2,
            grid=(steps,),
            in_specs=[place(other) for other in (0, 1, 0, 1)]
            + [pl.BlockSpec(memory_space=pl.ANY)] * len(kept),
            out_specs=(out_spec, out_spec),
        ),
        out_shape=(shape, shape),
        input_output_aliases={6 + number: number for number in range(len(kept))},
        compiler_params=limit(20),
        cost_estimate=estimate(0.02),
    )(core.reshape(1), sides, *pieces, *kept)


GELU_SCALE = (2.0 / 3.141592653589793) ** 0.5


def across(left, right):
    return lax.dot_general(
        left, right, (((1,), (1,)), ((), ())), preferred_element_type=jnp.float32
    )


def inner_rows(left, right):
    return lax.dot_general(
        left, right, (((0,), (0,)), ((), ())), preferred_element_type=jnp.float32
    )


def product(left, right):
    return jnp.dot(left, right, preferred_element_type=jnp.float32)


def normalized(values):
    center = values - jnp.mean(values, axis=-1, keepdims=True)
    spread = jnp.mean(center * center, axis=-1, keepdims=True)
    factor = lax.rsqrt(spread + norm_epsilon)
    return center * factor, factor


def norm_back(grad, normal, factor, gain):
    scaled = grad * gain
    mean_scaled = jnp.mean(scaled, axis=-1, keepdims=True)
    mean_normal = jnp.mean(scaled * normal, axis=-1, keepdims=True)
    return factor * (scaled - mean_scaled - normal * mean_normal)


def same_segment(layout_ref, row, length):
    def segment(axis):
        places = lax.broadcasted_iota(jnp.int32, (length, length), axis)
        total = jnp.zeros((length, length), jnp.int32)
        bound = 0
        for picture in range(3):
            bound = bound + layout_ref[row, picture]
            total = total + (places >= bound).astype(jnp.int32)
        return total

    return segment(0) == segment(1)


def head_probs(query, key, same):
    scores = inner_rows(query, key) * (HEAD ** (-0.5))
    scores = jnp.where(same, scores, -1000000000.0)
    exponent = jnp.exp(scores - jnp.max(scores, axis=-1, keepdims=True))
    return exponent / jnp.sum(exponent, axis=-1, keepdims=True)


def as_column(vector):
    return jnp.broadcast_to(vector[None, :], (8, vector.shape[0])).T[:, 0:1]


def lanes(count):
    return -(-count // 128) * 128


def whole(shape):
    return pl.BlockSpec(shape, lambda *_: (0,) * len(shape))


def scalars():
    return pl.BlockSpec(memory_space=pltpu.SMEM)


def estimate(microseconds):
    return pl.CostEstimate(
        flops=int(microseconds * 1.15e9), bytes_accessed=1024, transcendentals=0
    )


def limit(mebibytes):
    return pltpu.CompilerParams(vmem_limit_bytes=mebibytes * 1024 * 1024)


def low(values):
    return values.astype(jnp.bfloat16)


def attention_forward(row, layout, hidden, gain, shift, wq, bq, wk, wv, bv, wo):
    _, length, width = hidden.shape
    wide = wq.shape[0]

    def kernel(
        layout_ref, hidden_ref, gain_ref, shift_ref, wq_ref, bq_ref, wk_ref, wv_ref, bv_ref,
        wo_ref, normed_ref, q_ref, k_ref, v_ref, att_ref, branch_ref, normed_send_ref, att_send_ref,
    ):
        normal, _ = normalized(hidden_ref[0].astype(jnp.float32))
        normed = low(normal * gain_ref[...][None, :] + shift_ref[...][None, :])
        normed_ref[...] = normed
        normed_send_ref[...] = normed.astype(jnp.float32)
        queries = low(across(wq_ref[...], normed) + as_column(bq_ref[...]))
        keys = low(across(wk_ref[...], normed))
        values = low(across(wv_ref[...], normed) + as_column(bv_ref[...]))
        q_ref[...] = queries
        k_ref[...] = keys
        v_ref[...] = values
        queries, keys, values = (part.astype(jnp.float32) for part in (queries, keys, values))
        same = same_segment(layout_ref, row, length)
        parts = []
        for head in range(wide // HEAD):
            rows = slice(head * HEAD, (head + 1) * HEAD)
            probs = head_probs(low(queries[rows]), low(keys[rows]), same)
            parts.append(across(low(values[rows]), low(probs)))
        attended = low(jnp.concatenate(parts, 0))
        att_ref[...] = attended
        att_send_ref[:, :length] = attended.astype(jnp.float32)
        att_send_ref[:, length:] = jnp.zeros((wide, lanes(length) - length), jnp.float32)
        branch_ref[...] = inner_rows(attended, wo_ref[...])

    turned = jax.ShapeDtypeStruct((wide, length), jnp.bfloat16)
    return pl.pallas_call(
        kernel,
        grid=(1,),
        in_specs=[
            scalars(),
            pl.BlockSpec((1, length, width), lambda i: (row, 0, 0)),
            whole((width,)),
            whole((width,)),
            whole((wide, width)),
            whole((wide,)),
            whole((wide, width)),
            whole((wide, width)),
            whole((wide,)),
            whole((wide, width)),
        ],
        out_specs=[whole((length, width))]
        + [whole((wide, length))] * 4
        + [whole((length, width))] * 2
        + [whole((wide, lanes(length)))],
        out_shape=[
            jax.ShapeDtypeStruct((length, width), jnp.bfloat16),
            turned,
            turned,
            turned,
            turned,
            jax.ShapeDtypeStruct((length, width), jnp.float32),
            jax.ShapeDtypeStruct((length, width), jnp.float32),
            jax.ShapeDtypeStruct((wide, lanes(length)), jnp.float32),
        ],
        compiler_params=limit(56),
        cost_estimate=estimate(20),
    )(layout, hidden, gain, shift, wq, bq, wk, wv, bv, wo)


def attention_backward(row, core, layout, part, received, resid, cotangent, gain, q, k, v, wo):
    _, length, width = cotangent.shape
    wide = wo.shape[0]

    def kernel(
        core_ref, layout_ref, part_ref, received_ref, resid_ref, cot_ref, gain_ref, q_ref, k_ref, v_ref,
        wo_ref, resid_grad_ref, branch_grad_ref, terms_ref, dq_ref, dk_ref, dv_ref, send_ref,
        branch_send_ref,
    ):
        mid_grad = part_ref[...] + received_ref[...]
        normal, factor = normalized(resid_ref[...])
        terms_ref[0:1, :] = jnp.sum(mid_grad * normal, axis=0, keepdims=True)
        terms_ref[1:2, :] = jnp.sum(mid_grad, axis=0, keepdims=True)
        resid_grad = cot_ref[0].astype(jnp.float32) + norm_back(
            mid_grad, normal, factor, gain_ref[...][None, :]
        )
        resid_grad_ref[...] = resid_grad
        branch_grad = low(resid_grad)
        branch_grad_ref[...] = branch_grad
        branch_send_ref[...] = branch_grad.astype(jnp.float32)
        terms_ref[2:3, :] = jnp.sum(branch_grad.astype(jnp.float32), axis=0, keepdims=True)
        terms_ref[3:8, :] = jnp.zeros((5, width), jnp.float32)
        back = low(across(wo_ref[...], branch_grad)).astype(jnp.float32)
        same = same_segment(layout_ref, row, length)
        queries, keys, values = (
            ref[...].astype(jnp.float32) for ref in (q_ref, k_ref, v_ref)
        )
        dq, dk, dv = [], [], []
        for head in range(wide // HEAD):
            rows = slice(head * HEAD, (head + 1) * HEAD)
            query, key, value, grad = (
                low(member[rows]) for member in (queries, keys, values, back)
            )
            probs = head_probs(query, key, same)
            dv.append(product(grad, low(probs)))
            prob_grad = inner_rows(grad, value)
            inside = prob_grad - jnp.sum(prob_grad * probs, axis=-1, keepdims=True)
            score_grad = low(probs * inside)
            dq.append(across(key, score_grad) * (HEAD ** (-0.5)))
            dk.append(product(query, score_grad) * (HEAD ** (-0.5)))
        dq, dk, dv = (low(jnp.concatenate(parts, 0)) for parts in (dq, dk, dv))
        dq_ref[...] = dq
        dk_ref[...] = dk
        dv_ref[...] = dv
        send_ref[: 2 * wide, length:] = jnp.zeros((2 * wide, lanes(length) - length), jnp.float32)
        send_ref[wide : 2 * wide, :length] = dk.astype(jnp.float32)

        @pl.when(core_ref[0] == 0)
        def _():
            send_ref[:wide, :length] = dv.astype(jnp.float32)

        @pl.when(core_ref[0] != 0)
        def _():
            send_ref[:wide, :length] = dq.astype(jnp.float32)

    turned = jax.ShapeDtypeStruct((wide, length), jnp.bfloat16)
    return pl.pallas_call(
        kernel,
        grid=(1,),
        in_specs=[scalars(), scalars()]
        + [pl.BlockSpec((length, width), lambda i: (row, 0))] * 2
        + [whole((length, width))]
        + [pl.BlockSpec((1, length, width), lambda i: (row, 0, 0)), whole((width,))]
        + [whole((wide, length))] * 3
        + [whole((wide, width))],
        out_specs=[whole((length, width)), whole((length, width)), whole((8, width))]
        + [whole((wide, length))] * 3
        + [whole((2 * wide, lanes(length))), whole((length, width))],
        out_shape=[
            jax.ShapeDtypeStruct((length, width), jnp.float32),
            jax.ShapeDtypeStruct((length, width), jnp.bfloat16),
            jax.ShapeDtypeStruct((8, width), jnp.float32),
            turned,
            turned,
            turned,
            jax.ShapeDtypeStruct((2 * wide, lanes(length)), jnp.float32),
            jax.ShapeDtypeStruct((length, width), jnp.float32),
        ],
        compiler_params=limit(56),
        cost_estimate=estimate(0.02),
    )(core.reshape(1), layout, part, received, resid, cotangent, gain, q, k, v, wo)


def feed_forward(
    row, core, hidden, branch, received, out_bias, gain, shift, up, up_bias, down, cotangent,
    mid_parts=None,
):
    _, length, width = hidden.shape
    units = up.shape[0]
    kept = [] if mid_parts is None else [mid_parts]
    block = 576
    steps = -(-units // block)

    def kernel(
        core_ref, hidden_ref, branch_ref, received_ref, out_bias_ref, gain_ref, shift_ref, up_ref,
        up_bias_ref, down_ref, cot_ref, *refs,
    ):
        resid_ref, middle_ref, pair_ref, mid_part_ref, out_part_ref = refs[-7:-2]
        left_send_ref, right_send_ref = refs[-2:]
        step = pl.program_id(0)
        first_core = core_ref[0] == 0

        @pl.when(step == 0)
        def _():
            resid = hidden_ref[0].astype(jnp.float32) + (
                (branch_ref[...] + received_ref[...]) + out_bias_ref[...][None, :]
            )
            resid_ref[...] = resid
            normal, _ = normalized(resid)
            middle = low(normal * gain_ref[...][None, :] + shift_ref[...][None, :])
            middle_ref[...] = middle
            mid_part_ref[...] = jnp.zeros((length, width), jnp.float32)
            out_part_ref[...] = jnp.zeros((length, width), jnp.float32)

            @pl.when(first_core)
            def _():
                right_send_ref[...] = middle.astype(jnp.float32)

            @pl.when(jnp.logical_not(first_core))
            def _():
                right_send_ref[...] = cot_ref[0].astype(jnp.float32)

        def work(up_here, down_here, up_bias_here):
            act = across(up_here, middle_ref[...]) + up_bias_here
            act_grad = across(down_here, cot_ref[0])
            curve = jnp.tanh(GELU_SCALE * (act + 0.044715 * (act * act * act)))
            activ = low(0.5 * act * (1.0 + curve))
            slope = 0.5 * (1.0 + curve) + 0.5 * act * (1.0 - curve * curve) * (
                GELU_SCALE * (1.0 + 3.0 * 0.044715 * (act * act))
            )
            pre_grad = low(act_grad * slope)
            pair_ref[0] = activ
            pair_ref[1] = pre_grad
            left_send_ref[:, length:] = jnp.zeros((block, lanes(length) - length), jnp.float32)
            mid_part_ref[...] += inner_rows(pre_grad, up_here)
            out_part_ref[...] += inner_rows(activ, down_here)

            @pl.when(first_core)
            def _():
                left_send_ref[:, :length] = pre_grad.astype(jnp.float32)

            @pl.when(jnp.logical_not(first_core))
            def _():
                left_send_ref[:, :length] = activ.astype(jnp.float32)

        @pl.when(step < steps - 1)
        def _():
            work(up_ref[...], down_ref[...], up_bias_ref[...])

        @pl.when(step == steps - 1)
        def _():
            here = step * block + lax.broadcasted_iota(jnp.int32, (block, width), 0)
            inside = here < units
            work(
                low(jnp.where(inside, up_ref[...].astype(jnp.float32), 0.0)),
                low(jnp.where(inside, down_ref[...].astype(jnp.float32), 0.0)),
                jnp.where(inside[:, :1], up_bias_ref[...], 0.0),
            )

    flat = jax.ShapeDtypeStruct((length, width), jnp.float32)
    at_row = pl.BlockSpec((1, length, width), lambda i: (row, 0, 0))
    return pl.pallas_call(
        kernel,
        grid=(steps,),
        in_specs=[scalars(), at_row]
        + [whole((length, width))] * 2
        + [whole((width,))] * 3
        + [
            pl.BlockSpec((block, width), lambda i: (i, 0)),
            pl.BlockSpec((block, 1), lambda i: (i, 0)),
            pl.BlockSpec((block, width), lambda i: (i, 0)),
            at_row,
        ]
        + [pl.BlockSpec(memory_space=pl.ANY)] * len(kept),
        out_specs=[
            whole((length, width)),
            whole((length, width)),
            pl.BlockSpec((2, block, length), lambda i: (0, i, 0)),
            pl.BlockSpec((length, width), lambda i: (row, 0)),
            whole((length, width)),
            pl.BlockSpec((block, lanes(length)), lambda i: (i, 0)),
            whole((length, width)),
        ],
        out_shape=[
            flat,
            jax.ShapeDtypeStruct((length, width), jnp.bfloat16),
            jax.ShapeDtypeStruct((2, steps * block, length), jnp.bfloat16),
            jax.ShapeDtypeStruct((hidden.shape[0] * length, width), jnp.float32),
            flat,
            jax.ShapeDtypeStruct((steps * block, lanes(length)), jnp.float32),
            flat,
        ],
        input_output_aliases={11 + number: 3 for number in range(len(kept))},
        compiler_params=limit(56),
        cost_estimate=estimate(30),
    )(
        core.reshape(1), hidden, branch, received, out_bias, gain, shift, up, up_bias, down,
        cotangent, *kept,
    )


def ff_own(core, sides, pairs, cotangent, middles, lefts, rights, counts, base):
    rows = len(pairs)
    length, columns = middles[0].shape
    streams = len(counts)
    units = sum(counts)
    firsts = [sum(counts[:number]) for number in range(streams)]
    part = base // units

    def kernel(core_ref, sides_ref, *refs):
        pair_refs = refs[:rows]
        cot_ref = refs[rows]
        middle_refs = refs[rows + 1 : 2 * rows + 1]
        left_refs = refs[2 * rows + 1 : 3 * rows + 1]
        right_refs = refs[3 * rows + 1 : 4 * rows + 1]
        out_refs = refs[4 * rows + 1 : 4 * rows + 1 + 2 * streams]
        own_ref, other_ref = refs[4 * rows + 1 + 2 * streams :]
        step = pl.program_id(0)

        @pl.when(step == 0)
        def _():
            for row in range(rows):
                other_ref[row] = low(right_refs[row][...])

        @pl.when((step == 0) & (core_ref[0] == 0))
        def _():
            for row in range(rows):
                own_ref[row] = cot_ref[row]

        @pl.when((step == 0) & (core_ref[0] != 0))
        def _():
            for row in range(rows):
                own_ref[row] = middle_refs[row][...]

        for number in range(streams):
            half = counts[number] // 2
            for keep in range(2):

                @pl.when(step == keep * streams + number)
                def _():
                    here = sides_ref[number] if keep else 1 - sides_ref[number]
                    here = pl.ds(pl.multiple_of(firsts[number] + here * half, 16), half)
                    total = product(pair_refs[0][0, here, :], own_ref[0])
                    for row in range(1, rows):
                        total = total + product(pair_refs[row][0, here, :], own_ref[row])
                    for row in range(rows):
                        left = low(left_refs[row][here, :length])
                        total = total + product(left, other_ref[row])
                    out_refs[2 * number + keep][...] = total

    shapes = [
        jax.ShapeDtypeStruct((count // 2, columns), jnp.float32)
        for count in counts
        for _ in range(2)
    ]
    return pl.pallas_call(
        kernel,
        grid_spec=pltpu.PrefetchScalarGridSpec(
            num_scalar_prefetch=2,
            grid=(2 * streams,),
            in_specs=[
                pl.BlockSpec((1, units, length), lambda step, core_ref, _: (core_ref[0], part, 0))
            ]
            * rows
            + [whole(cotangent.shape)]
            + [whole((length, columns))] * rows
            + [pl.BlockSpec((units, lanes(length)), lambda step, core_ref, _: (part, 0))] * rows
            + [whole((length, columns))] * rows,
            out_specs=[whole(shape.shape) for shape in shapes],
            scratch_shapes=[pltpu.VMEM((rows, length, columns), jnp.bfloat16)] * 2,
        ),
        out_shape=shapes,
        compiler_params=limit(56),
        cost_estimate=estimate(4),
    )(core.reshape(1), sides, *pairs, cotangent, *middles, *lefts, *rights)


def attention_own(core, dq, dk, dv, attended, normed, branch_grad, early, late):
    rows = len(dq)
    wide, length = dq[0].shape
    columns = normed[0].shape[1]
    piece = wide // 2

    def kernel(core_ref, *refs):
        groups = [refs[rows * number : rows * (number + 1)] for number in range(10)]
        dq_refs, dk_refs, dv_refs, attended_refs, normed_refs, branch_refs = groups[:6]
        early_normed, early_attended, late_refs, late_branch = groups[6:]
        out_ref = refs[10 * rows]
        step = pl.program_id(0)
        first_core = core_ref[0] == 0
        late_step = step >= 2

        def store(lefts, rights, other_lefts, other_rights):
            total = product(lefts[0][...], rights[0][...])
            for row in range(1, rows):
                total = total + product(lefts[row][...], rights[row][...])
            for row in range(rows):
                total = total + product(low(other_lefts[row]), low(other_rights[row]))
            out_ref[...] = total

        late_left = [
            ref[pl.ds(pl.multiple_of(step * piece, 16), piece), :length] for ref in late_refs
        ]

        @pl.when(jnp.logical_not(late_step) & first_core)
        def _():
            store(dq_refs, normed_refs, late_left, [ref[...] for ref in early_normed])

        @pl.when(late_step & first_core)
        def _():
            store(dk_refs, normed_refs, late_left, [ref[...] for ref in early_normed])

        @pl.when(jnp.logical_not(late_step) & jnp.logical_not(first_core))
        def _():
            store(dv_refs, normed_refs, late_left, [ref[...] for ref in early_normed])

        @pl.when(late_step & jnp.logical_not(first_core))
        def _():
            store(
                attended_refs,
                branch_refs,
                [ref[:, :length] for ref in early_attended],
                [ref[...] for ref in late_branch],
            )

    def first_half(wide_here):
        return pl.BlockSpec((piece, wide_here), lambda step, core_ref: (jnp.minimum(step, 1), 0))

    def second_half(wide_here):
        return pl.BlockSpec(
            (piece, wide_here), lambda step, core_ref: (jnp.maximum(step - 2, 0), 0)
        )

    wholes = [whole((length, columns))] * rows
    return pl.pallas_call(
        kernel,
        grid_spec=pltpu.PrefetchScalarGridSpec(
            num_scalar_prefetch=1,
            grid=(4,),
            in_specs=([first_half(length)] * rows + [second_half(length)] * rows) * 2
            + wholes * 2
            + wholes
            + [second_half(lanes(length))] * rows
            + [whole(late[0][0].shape)] * rows
            + wholes,
            out_specs=pl.BlockSpec((piece, columns), lambda step, core_ref: (step, 0)),
        ),
        out_shape=jax.ShapeDtypeStruct((2 * wide, columns), jnp.float32),
        compiler_params=limit(56),
        cost_estimate=estimate(0.02),
    )(
        core.reshape(1), *dq, *dk, *dv, *attended, *normed, *branch_grad,
        *[member for place in range(2) for member in [part[place] for part in early]],
        *[member for place in range(2) for member in [part[place] for part in late]],
    )


def shards(
    hidden_in,
    row_layout,
    cotangent,
    pre_gain,
    pre_shift,
    query_weight,
    query_bias,
    key_weight,
    value_weight,
    value_bias,
    out_weight,
    out_bias,
    mid_gain,
    mid_shift,
    up_weight,
    up_bias,
    down_weight,
    down_bias,
):
    rows, length, width = hidden_in.shape
    tokens = rows * length
    heads_wide = query_weight.shape[1]
    hidden = up_weight.shape[1]
    side = sides()
    core = side["core"]
    order = Order()
    query_turned = query_weight.T
    key_turned = key_weight.T
    value_turned = value_weight.T
    up_turned = up_weight.T

    forward = [
        order.run(
            lambda ready: attention_forward(
                row, row_layout, ready, pre_gain, pre_shift, query_turned, query_bias, key_turned,
                value_turned, value_bias, out_weight,
            ),
            hidden_in,
        )
        for row in range(rows)
    ]

    up_column = up_bias.reshape(-1, 1)
    middle = []
    early = []
    for row in range(rows):
        if row > 0:
            with jax.named_scope("early_core_move_" + str(row - 1)):
                early.append(order.settle([swap(forward[row - 1].value[n], "core") for n in (6, 7)]))
        with jax.named_scope("branch_move_" + str(row)):
            received = swap_tensor(forward[row].value[5])
        middle.append(
            order.run(
                lambda ready: feed_forward(
                    row, core, hidden_in, ready, received, out_bias, mid_gain, mid_shift,
                    up_turned, up_column, down_weight, cotangent,
                    None if row == 0 else middle[row - 1].value[3],
                ),
                forward[row].value[5],
            )
        )
    with jax.named_scope("early_core_move_" + str(rows - 1)):
        early.append(order.settle([swap(forward[rows - 1].value[n], "core") for n in (6, 7)]))
    normed = [forward[row].value[0] for row in range(rows)]
    attended = [forward[row].value[4] for row in range(rows)]
    resid = [middle[row].value[0] for row in range(rows)]
    middles = [middle[row].value[1] for row in range(rows)]
    backward = []

    def back(row, received):
        _, q, k, v = forward[row].value[:4]
        backward.append(
            order.run(
                lambda ready: attention_backward(
                    row, core, row_layout, ready, received, resid[row], cotangent, mid_gain,
                    q, k, v, out_weight,
                ),
                middle[rows - 1].value[3],
            )
        )

    pairs = [middle[row].value[2] for row in range(rows)]
    ff_rows = (576, 576, 576, 576)
    ff_streams = [Stream("ff" + str(n), order, ORDERS[n], side) for n in range(4)]

    def ff_step(extra=None):
        moved = [stream.moved() for stream in ff_streams]
        received = lax.optimization_barrier(moved + ([] if extra is None else [extra]))
        for stream, part in zip(ff_streams, received):
            stream.step(part)
        return received[-1]

    lefts, rights = [], []

    def ff_core_move(row):
        with jax.named_scope("ff_core_move_" + str(row)):
            lefts.append(swap(middle[row].value[5], "core"))
            rights.append(swap(middle[row].value[6], "core"))

    ff_core_move(0)
    lefts[0] = order.settle(lefts[0])
    rights[0] = order.settle(rights[0])
    ff_core_move(1)
    ff_sides = jnp.stack([side[stream.pairs[0]] for stream in ff_streams])

    def ff_begin(first):
        members = ff_streams[first : first + 2]
        halves = order.run(
            lambda ready: ff_own(
                core, ff_sides[first : first + 2], [pairs[0], ready], cotangent, middles, lefts,
                rights, ff_rows[first : first + 2], sum(ff_rows[:first]),
            ),
            pairs[1],
        )
        for n, stream in enumerate(members):
            stream.begin(*halves.value[2 * n : 2 * n + 2])

    ff_begin(0)
    ff_begin(2)
    with jax.named_scope("mid_move"):
        mid_received = swap_tensor(middle[rows - 1].value[3])
    back(0, mid_received)
    back(1, mid_received)

    dq, dk, dv = ([backward[row].value[place] for row in range(rows)] for place in (3, 4, 5))
    branch_grad = [backward[row].value[1] for row in range(rows)]
    output = []

    def output_move(row):
        with jax.named_scope("output_move_" + str(row)):
            return swap_tensor(middle[row].value[4])

    def output_row(row, received):
        output.append(
            order.run(
                lambda ready: low(resid[row] + (ready + received) + down_bias),
                middle[row].value[4],
            )
        )

    def normed_move(row):
        with jax.named_scope("normed_move_" + str(row)):
            return swap_tensor(normed_part[row].value)

    output_row(0, ff_step(output_move(0)))
    late = []
    for row in range(rows):
        with jax.named_scope("late_core_move_" + str(row)):
            late.append(order.settle([swap(backward[row].value[n], "core") for n in (6, 7)]))
    at_own = order.run(
        lambda ready: attention_own(
            core, [dq[0], ready], dk, dv, attended, normed, branch_grad, early, late
        ),
        dq[1],
    )
    with jax.named_scope("at_scatter"):
        at_block = lax.psum_scatter(
            at_own.value, "dp", axis_index_groups=PLANES, scatter_dimension=0, tiled=True
        )
    normed_part = [
        order.run(
            lambda ready: inner_rows(ready, query_turned)
            + inner_rows(dk[row], key_turned)
            + inner_rows(dv[row], value_turned),
            dq[row],
        )
        for row in range(rows)
    ]
    ff_step()
    normed_received = [ff_step(normed_move(0))]
    normed_received.append(ff_step(normed_move(1)))
    normed_grad = order.run(
        lambda ready: jnp.concatenate(
            [ready + normed_received[0], normed_part[1].value + normed_received[1]], 0
        ),
        normed_part[0].value,
    )
    pre_normal, pre_factor = normalized(hidden_in.reshape(tokens, width).astype(jnp.float32))
    pre_gain_grad = jnp.sum(normed_grad.value * pre_normal, axis=0)
    pre_shift_grad = jnp.sum(normed_grad.value, axis=0)
    resid_grad = jnp.concatenate([backward[row].value[0] for row in range(rows)], 0)
    input_grad = resid_grad + norm_back(normed_grad.value, pre_normal, pre_factor, pre_gain)
    terms = sum(backward[row].value[2] for row in range(rows))

    def token_sum(members):
        return sum(jnp.sum(member.astype(jnp.float32), axis=1) for member in members)

    small = jnp.concatenate(
        [
            pre_gain_grad,
            pre_shift_grad,
            terms[2],
            terms[0],
            terms[1],
            jnp.sum(cotangent.astype(jnp.float32), axis=(0, 1)),
            token_sum(dq),
            token_sum(dv),
            token_sum([pair[1, :hidden] for pair in pairs]),
            jnp.zeros((2 * width - hidden,), jnp.float32),
        ]
    ).reshape(9, width)
    small = order.run(lambda ready: ready, small)

    def small_move(pair):
        with jax.named_scope("small_move_" + pair):
            return swap(small.value, pair)

    def small_add(received):
        return order.run(lambda ready: ready + received, small.value)

    small = small_add(ff_step(small_move("z")))
    small = small_add(ff_step(small_move("xa")))
    small = small_add(ff_step(small_move("ya")))
    at_block = order.run(lambda ready: ready + 0.0, at_block)
    with jax.named_scope("at_z_move"):
        received = swap(at_block.value, "z")
    received = ff_step(received)
    halves = [stream.halves() for stream in ff_streams]
    at_block = order.run(lambda ready: ready + received, at_block.value)
    with jax.named_scope("at_gather"):
        at_whole = lax.all_gather(
            at_block.value, "dp", axis_index_groups=PLANES, axis=0, tiled=True
        )
    others = order.settle([other for _, other in halves] + [output_move(1)])
    output_row(1, others.pop())
    far = []
    for number, other in enumerate(others):
        with jax.named_scope("ff_core_other_" + str(number)):
            far.append((swap(halves[number][0], "core"), swap(other, "core")))
    down_up = None
    for n in range(4):
        down_up = pick_halves(
            core, ff_sides[n : n + 1], (halves[n][0], others[n], *far[n]), hidden,
            sum(ff_rows[:n]), down_up,
        )
        first_down, small.value = lax.optimization_barrier((down_up[0], small.value))
        down_up = (first_down, down_up[1])
        if n < 3:
            small = small_add(small_move(("xb", "yb", "core")[n]))
    down_grad, up_grad = down_up
    input_low, small.value, at_whole, down_grad = lax.optimization_barrier(
        (low(input_grad), small.value, at_whole, down_grad)
    )
    with jax.named_scope("at_core_back"):
        received = swap(at_whole, "core")
    query_weight_grad, value_weight_grad = pick_rows(
        core, at_whole, received, heads_wide, 192, 0, 0, heads_wide
    )
    key_weight_grad, out_grad = pick_rows(
        core, at_whole, received, heads_wide, 192, heads_wide, 0, heads_wide
    )
    small = small.value
    return (
        jnp.stack([part.value for part in output]),
        input_low.reshape(hidden_in.shape),
        small[0],
        small[1],
        query_weight_grad.T,
        small[6, :heads_wide],
        key_weight_grad.T,
        value_weight_grad.T,
        small[6, heads_wide:],
        out_grad,
        small[2],
        small[3],
        small[4],
        up_grad.T,
        small[7:].reshape(-1)[:hidden],
        down_grad,
        small[5],
    )


def solution(mesh):
    placed = (
        P("dp", None, None),
        P("dp", None),
        P("dp", None, None),
        P(),
        P(),
        P(None, "tensor"),
        P("tensor"),
        P(None, "tensor"),
        P(None, "tensor"),
        P("tensor"),
        P("tensor", None),
        P(),
        P(),
        P(),
        P(None, "tensor"),
        P("tensor"),
        P("tensor", None),
        P(),
    )
    return jax.shard_map(
        shards,
        mesh=mesh,
        in_specs=placed,
        out_specs=(
            P("dp", None, None),
            P("dp", None, None),
            P(),
            P(),
            P(None, "tensor"),
            P("tensor"),
            P(None, "tensor"),
            P(None, "tensor"),
            P("tensor"),
            P("tensor", None),
            P(),
            P(),
            P(),
            P(None, "tensor"),
            P("tensor"),
            P("tensor", None),
            P(),
        ),
        check_vma=False,
    )
```

```python
import jax
import jax.numpy as jnp
from jax import lax
from jax.experimental import pallas as pl
from jax.experimental.pallas import tpu as pltpu
from jax.sharding import PartitionSpec as P

HEAD = 72
norm_epsilon = 1e-06


def partner_pairs(move):
    pairs = []
    for place in range(64):
        z_hi, x, y, core = place >> 5, (place >> 3) & 3, (place >> 1) & 3, place & 1
        z_hi, x, y, core = move(z_hi, x, y, core)
        pairs.append((place, ((z_hi * 4 + x) * 4 + y) * 2 + core))
    return pairs


PAIRS = {
    "core": partner_pairs(lambda z, x, y, c: (z, x, y, 1 - c)),
    "xa": partner_pairs(lambda z, x, y, c: (z, x ^ 1, y, c)),
    "xb": partner_pairs(lambda z, x, y, c: (z, x ^ 3, y, c)),
    "ya": partner_pairs(lambda z, x, y, c: (z, x, y ^ 1, c)),
    "yb": partner_pairs(lambda z, x, y, c: (z, x, y ^ 3, c)),
    "z": partner_pairs(lambda z, x, y, c: (1 - z, x, y, c)),
}
PLANES = [
    [((z_hi * 4 + x) * 4 + y) * 2 + core for x in range(4) for y in range(4)]
    for z_hi in range(2)
    for core in range(2)
]
ORDERS = (
    ("xa", "ya", "xb", "yb"),
    ("ya", "xb", "yb", "xa"),
    ("xb", "yb", "xa", "ya"),
    ("yb", "xa", "ya", "xb"),
)


def sides():
    place = lax.axis_index("dp")
    x = (place >> 3) & 3
    y = (place >> 1) & 3
    return {
        "core": place & 1,
        "xa": (x ^ (x >> 1)) & 1,
        "xb": x >> 1,
        "ya": (y ^ (y >> 1)) & 1,
        "yb": y >> 1,
    }


def swap(values, pair):
    return lax.ppermute(values, "dp", PAIRS[pair])


def swap_tensor(values):
    return lax.ppermute(values, "tensor", [(0, 1), (1, 0)])


class Cell:
    def __init__(self, value):
        self.value = value


class Order:
    def __init__(self):
        self.last = None

    def run(self, operation, ready):
        if self.last is not None:
            self.last.value, ready = lax.optimization_barrier((self.last.value, ready))
        self.last = Cell(operation(ready))
        return self.last

    def settle(self, value):
        self.last.value, value = lax.optimization_barrier((self.last.value, value))
        return value


def half_of(values, side):
    count = values.shape[0] // 2
    return lax.dynamic_slice_in_dim(values, side * count, count, 0)


def row_half_of(values, side):
    count = values.shape[1] // 2
    return jnp.where(side == 0, values[:, :count], values[:, count:])


def joined(own, received, side, axis):
    return jnp.where(
        side == 0,
        jnp.concatenate([own, received], axis),
        jnp.concatenate([received, own], axis),
    )


class Stream:
    def __init__(self, name, order, pairs, side):
        self.name = name
        self.order = order
        self.pairs = pairs
        self.side = side
        self.stage = 0
        self.keep = None
        self.sent = None

    def begin(self, send, keep):
        four = (4, send.shape[0] // 4, send.shape[1])
        self.sent = Cell(send.reshape(four))
        self.order.last = self.sent
        self.keep = keep.reshape(four)
        self.stage = 1

    def moved(self):
        pairs = self.pairs
        stage = self.stage
        with jax.named_scope(self.name + "_move_" + str(stage)):
            if stage <= 4:
                return swap(self.sent.value, pairs[stage - 1])
            if stage == 5:
                return swap(self.sent.value, "z")
            return swap(self.sent.value, pairs[9 - stage])

    def step(self, received):
        pairs = self.pairs
        stage = self.stage
        self.stage += 1
        keep = self.keep
        with jax.named_scope(self.name + "_sum_" + str(stage)):
            if stage <= 3:
                take = half_of if stage < 3 else row_half_of
                side = self.side[pairs[stage]]
                self.keep = take(keep, side) + take(received, side)
                self.sent = self.order.run(
                    lambda ready: take(ready, 1 - side) + take(received, 1 - side), keep
                )
            elif stage == 4:
                self.sent = self.order.run(lambda ready: ready + received, keep)
            elif stage == 5:
                self.sent = self.order.run(lambda ready: ready + received, self.sent.value)
            else:
                axis = 1 if stage == 6 else 0
                pair = pairs[9 - stage]
                self.sent = self.order.run(
                    lambda ready: joined(ready, received, self.side[pair], axis), self.sent.value
                )

    def halves(self):
        here = self.sent.value
        flat = (-1, here.shape[2])
        return here.reshape(flat), self.moved().reshape(flat)


def pick_rows(core, own, other, rows, block, skipped, first, total, kept=()):
    columns = own.shape[1]
    before, start = skipped // block, first // block

    def kernel(core_ref, own_ref, other_ref, *refs):
        first_ref, second_ref = refs[-2:]

        @pl.when(core_ref[0] == 0)
        def _():
            first_ref[...] = own_ref[...]
            second_ref[...] = other_ref[...]

        @pl.when(core_ref[0] != 0)
        def _():
            first_ref[...] = other_ref[...]
            second_ref[...] = own_ref[...]

    shape = jax.ShapeDtypeStruct((total, columns), jnp.float32)
    in_spec = pl.BlockSpec((block, columns), lambda i, core_ref: (before + i, 0))
    out_spec = pl.BlockSpec((block, columns), lambda i, core_ref: (start + i, 0))
    return pl.pallas_call(
        kernel,
        grid_spec=pltpu.PrefetchScalarGridSpec(
            num_scalar_prefetch=1,
            grid=(-(-rows // block),),
            in_specs=[in_spec, in_spec] + [pl.BlockSpec(memory_space=pl.ANY)] * len(kept),
            out_specs=(out_spec, out_spec),
        ),
        out_shape=(shape, shape),
        input_output_aliases={3 + number: number for number in range(len(kept))},
        compiler_params=limit(20),
        cost_estimate=estimate(8),
    )(core.reshape(1), own, other, *kept)


def pick_halves(core, sides, pieces, rows, first, before):
    half, columns = pieces[0].shape
    block = half // 2
    start = first // block

    def kernel(core_ref, sides_ref, *refs):
        first_ref, second_ref = refs[-2:]
        here = (pl.program_id(0) // 2) == sides_ref[0]
        for other in range(2):
            own_ref, far_ref = refs[other], refs[2 + other]
            chosen = here if other == 0 else jnp.logical_not(here)

            @pl.when(chosen & (core_ref[0] == 0))
            def _():
                first_ref[...] = own_ref[...]
                second_ref[...] = far_ref[...]

            @pl.when(chosen & (core_ref[0] != 0))
            def _():
                first_ref[...] = far_ref[...]
                second_ref[...] = own_ref[...]

    def place(other):
        def index(i, core_ref, sides_ref):
            side = sides_ref[0] if other == 0 else 1 - sides_ref[0]
            return (jnp.clip(i - side * 2, 0, 1), 0)

        return pl.BlockSpec((block, columns), index)

    shape = jax.ShapeDtypeStruct((rows, columns), jnp.float32)
    out_spec = pl.BlockSpec((block, columns), lambda i, core_ref, sides_ref: (start + i, 0))
    steps = min(4, -(-(rows - first) // block))
    kept = [] if before is None else list(before)
    return pl.pallas_call(
        kernel,
        grid_spec=pltpu.PrefetchScalarGridSpec(
            num_scalar_prefetch=2,
            grid=(steps,),
            in_specs=[place(other) for other in (0, 1, 0, 1)]
            + [pl.BlockSpec(memory_space=pl.ANY)] * len(kept),
            out_specs=(out_spec, out_spec),
        ),
        out_shape=(shape, shape),
        input_output_aliases={6 + number: number for number in range(len(kept))},
        compiler_params=limit(20),
        cost_estimate=estimate(4),
    )(core.reshape(1), sides, *pieces, *kept)


GELU_SCALE = (2.0 / 3.141592653589793) ** 0.5


def across(left, right):
    return lax.dot_general(
        left, right, (((1,), (1,)), ((), ())), preferred_element_type=jnp.float32
    )


def inner_rows(left, right):
    return lax.dot_general(
        left, right, (((0,), (0,)), ((), ())), preferred_element_type=jnp.float32
    )


def product(left, right):
    return jnp.dot(left, right, preferred_element_type=jnp.float32)


def normalized(values):
    center = values - jnp.mean(values, axis=-1, keepdims=True)
    spread = jnp.mean(center * center, axis=-1, keepdims=True)
    factor = lax.rsqrt(spread + norm_epsilon)
    return center * factor, factor


def norm_back(grad, normal, factor, gain):
    scaled = grad * gain
    mean_scaled = jnp.mean(scaled, axis=-1, keepdims=True)
    mean_normal = jnp.mean(scaled * normal, axis=-1, keepdims=True)
    return factor * (scaled - mean_scaled - normal * mean_normal)


def same_segment(layout_ref, row, length):
    def segment(axis):
        places = lax.broadcasted_iota(jnp.int32, (length, length), axis)
        total = jnp.zeros((length, length), jnp.int32)
        bound = 0
        for picture in range(3):
            bound = bound + layout_ref[row, picture]
            total = total + (places >= bound).astype(jnp.int32)
        return total

    return segment(0) == segment(1)


def head_probs(query, key, same):
    scores = inner_rows(query, key) * (HEAD ** (-0.5))
    scores = jnp.where(same, scores, -1000000000.0)
    exponent = jnp.exp(scores - jnp.max(scores, axis=-1, keepdims=True))
    return exponent / jnp.sum(exponent, axis=-1, keepdims=True)


def as_column(vector):
    return jnp.broadcast_to(vector[None, :], (8, vector.shape[0])).T[:, 0:1]


def lanes(count):
    return -(-count // 128) * 128


def whole(shape):
    return pl.BlockSpec(shape, lambda *_: (0,) * len(shape))


def scalars():
    return pl.BlockSpec(memory_space=pltpu.SMEM)


def estimate(microseconds):
    return pl.CostEstimate(
        flops=int(microseconds * 1.15e9), bytes_accessed=1024, transcendentals=0
    )


def limit(mebibytes):
    return pltpu.CompilerParams(vmem_limit_bytes=mebibytes * 1024 * 1024)


def low(values):
    return values.astype(jnp.bfloat16)


def attention_forward(row, layout, hidden, gain, shift, wq, bq, wk, wv, bv, wo):
    _, length, width = hidden.shape
    wide = wq.shape[0]

    def kernel(
        layout_ref, hidden_ref, gain_ref, shift_ref, wq_ref, bq_ref, wk_ref, wv_ref, bv_ref,
        wo_ref, normed_ref, q_ref, k_ref, v_ref, att_ref, branch_ref, normed_send_ref, att_send_ref,
    ):
        normal, _ = normalized(hidden_ref[0].astype(jnp.float32))
        normed = low(normal * gain_ref[...][None, :] + shift_ref[...][None, :])
        normed_ref[...] = normed
        normed_send_ref[...] = normed.astype(jnp.float32)
        queries = low(across(wq_ref[...], normed) + as_column(bq_ref[...]))
        keys = low(across(wk_ref[...], normed))
        values = low(across(wv_ref[...], normed) + as_column(bv_ref[...]))
        q_ref[...] = queries
        k_ref[...] = keys
        v_ref[...] = values
        queries, keys, values = (part.astype(jnp.float32) for part in (queries, keys, values))
        same = same_segment(layout_ref, row, length)
        parts = []
        for head in range(wide // HEAD):
            rows = slice(head * HEAD, (head + 1) * HEAD)
            probs = head_probs(low(queries[rows]), low(keys[rows]), same)
            parts.append(across(low(values[rows]), low(probs)))
        attended = low(jnp.concatenate(parts, 0))
        att_ref[...] = attended
        att_send_ref[:, :length] = attended.astype(jnp.float32)
        att_send_ref[:, length:] = jnp.zeros((wide, lanes(length) - length), jnp.float32)
        branch_ref[...] = inner_rows(attended, wo_ref[...])

    turned = jax.ShapeDtypeStruct((wide, length), jnp.bfloat16)
    return pl.pallas_call(
        kernel,
        grid=(1,),
        in_specs=[
            scalars(),
            pl.BlockSpec((1, length, width), lambda i: (row, 0, 0)),
            whole((width,)),
            whole((width,)),
            whole((wide, width)),
            whole((wide,)),
            whole((wide, width)),
            whole((wide, width)),
            whole((wide,)),
            whole((wide, width)),
        ],
        out_specs=[whole((length, width))]
        + [whole((wide, length))] * 4
        + [whole((length, width))] * 2
        + [whole((wide, lanes(length)))],
        out_shape=[
            jax.ShapeDtypeStruct((length, width), jnp.bfloat16),
            turned,
            turned,
            turned,
            turned,
            jax.ShapeDtypeStruct((length, width), jnp.float32),
            jax.ShapeDtypeStruct((length, width), jnp.float32),
            jax.ShapeDtypeStruct((wide, lanes(length)), jnp.float32),
        ],
        compiler_params=limit(56),
        cost_estimate=estimate(20),
    )(layout, hidden, gain, shift, wq, bq, wk, wv, bv, wo)


def attention_backward(row, core, layout, part, received, resid, cotangent, gain, q, k, v, wo):
    _, length, width = cotangent.shape
    wide = wo.shape[0]

    def kernel(
        core_ref, layout_ref, part_ref, received_ref, resid_ref, cot_ref, gain_ref, q_ref, k_ref, v_ref,
        wo_ref, resid_grad_ref, branch_grad_ref, terms_ref, dq_ref, dk_ref, dv_ref, send_ref,
        branch_send_ref,
    ):
        mid_grad = part_ref[...] + received_ref[...]
        normal, factor = normalized(resid_ref[...])
        terms_ref[0:1, :] = jnp.sum(mid_grad * normal, axis=0, keepdims=True)
        terms_ref[1:2, :] = jnp.sum(mid_grad, axis=0, keepdims=True)
        resid_grad = cot_ref[0].astype(jnp.float32) + norm_back(
            mid_grad, normal, factor, gain_ref[...][None, :]
        )
        resid_grad_ref[...] = resid_grad
        branch_grad = low(resid_grad)
        branch_grad_ref[...] = branch_grad
        branch_send_ref[...] = branch_grad.astype(jnp.float32)
        terms_ref[2:3, :] = jnp.sum(branch_grad.astype(jnp.float32), axis=0, keepdims=True)
        terms_ref[3:8, :] = jnp.zeros((5, width), jnp.float32)
        back = low(across(wo_ref[...], branch_grad)).astype(jnp.float32)
        same = same_segment(layout_ref, row, length)
        queries, keys, values = (
            ref[...].astype(jnp.float32) for ref in (q_ref, k_ref, v_ref)
        )
        dq, dk, dv = [], [], []
        for head in range(wide // HEAD):
            rows = slice(head * HEAD, (head + 1) * HEAD)
            query, key, value, grad = (
                low(member[rows]) for member in (queries, keys, values, back)
            )
            probs = head_probs(query, key, same)
            dv.append(product(grad, low(probs)))
            prob_grad = inner_rows(grad, value)
            inside = prob_grad - jnp.sum(prob_grad * probs, axis=-1, keepdims=True)
            score_grad = low(probs * inside)
            dq.append(across(key, score_grad) * (HEAD ** (-0.5)))
            dk.append(product(query, score_grad) * (HEAD ** (-0.5)))
        dq, dk, dv = (low(jnp.concatenate(parts, 0)) for parts in (dq, dk, dv))
        dq_ref[...] = dq
        dk_ref[...] = dk
        dv_ref[...] = dv
        send_ref[: 2 * wide, length:] = jnp.zeros((2 * wide, lanes(length) - length), jnp.float32)
        send_ref[wide : 2 * wide, :length] = dk.astype(jnp.float32)

        @pl.when(core_ref[0] == 0)
        def _():
            send_ref[:wide, :length] = dv.astype(jnp.float32)

        @pl.when(core_ref[0] != 0)
        def _():
            send_ref[:wide, :length] = dq.astype(jnp.float32)

    turned = jax.ShapeDtypeStruct((wide, length), jnp.bfloat16)
    return pl.pallas_call(
        kernel,
        grid=(1,),
        in_specs=[scalars(), scalars()]
        + [pl.BlockSpec((length, width), lambda i: (row, 0))] * 2
        + [whole((length, width))]
        + [pl.BlockSpec((1, length, width), lambda i: (row, 0, 0)), whole((width,))]
        + [whole((wide, length))] * 3
        + [whole((wide, width))],
        out_specs=[whole((length, width)), whole((length, width)), whole((8, width))]
        + [whole((wide, length))] * 3
        + [whole((2 * wide, lanes(length))), whole((length, width))],
        out_shape=[
            jax.ShapeDtypeStruct((length, width), jnp.float32),
            jax.ShapeDtypeStruct((length, width), jnp.bfloat16),
            jax.ShapeDtypeStruct((8, width), jnp.float32),
            turned,
            turned,
            turned,
            jax.ShapeDtypeStruct((2 * wide, lanes(length)), jnp.float32),
            jax.ShapeDtypeStruct((length, width), jnp.float32),
        ],
        compiler_params=limit(56),
        cost_estimate=estimate(0.02),
    )(core.reshape(1), layout, part, received, resid, cotangent, gain, q, k, v, wo)


def feed_forward(
    row, core, hidden, branch, received, out_bias, gain, shift, up, up_bias, down, cotangent,
    mid_parts=None,
):
    _, length, width = hidden.shape
    units = up.shape[0]
    kept = [] if mid_parts is None else [mid_parts]
    block = 768
    steps = -(-units // block)

    def kernel(
        core_ref, hidden_ref, branch_ref, received_ref, out_bias_ref, gain_ref, shift_ref, up_ref,
        up_bias_ref, down_ref, cot_ref, *refs,
    ):
        resid_ref, middle_ref, pair_ref, mid_part_ref, out_part_ref = refs[-7:-2]
        left_send_ref, right_send_ref = refs[-2:]
        step = pl.program_id(0)
        first_core = core_ref[0] == 0

        @pl.when(step == 0)
        def _():
            resid = hidden_ref[0].astype(jnp.float32) + (
                (branch_ref[...] + received_ref[...]) + out_bias_ref[...][None, :]
            )
            resid_ref[...] = resid
            normal, _ = normalized(resid)
            middle = low(normal * gain_ref[...][None, :] + shift_ref[...][None, :])
            middle_ref[...] = middle
            mid_part_ref[...] = jnp.zeros((length, width), jnp.float32)
            out_part_ref[...] = jnp.zeros((length, width), jnp.float32)

            @pl.when(first_core)
            def _():
                right_send_ref[...] = middle.astype(jnp.float32)

            @pl.when(jnp.logical_not(first_core))
            def _():
                right_send_ref[...] = cot_ref[0].astype(jnp.float32)

        def work(up_here, down_here, up_bias_here):
            act = across(up_here, middle_ref[...]) + up_bias_here
            act_grad = across(down_here, cot_ref[0])
            curve = jnp.tanh(GELU_SCALE * (act + 0.044715 * (act * act * act)))
            activ = low(0.5 * act * (1.0 + curve))
            slope = 0.5 * (1.0 + curve) + 0.5 * act * (1.0 - curve * curve) * (
                GELU_SCALE * (1.0 + 3.0 * 0.044715 * (act * act))
            )
            pre_grad = low(act_grad * slope)
            pair_ref[0] = activ
            pair_ref[1] = pre_grad
            left_send_ref[:, length:] = jnp.zeros((block, lanes(length) - length), jnp.float32)
            mid_part_ref[...] += inner_rows(pre_grad, up_here)
            out_part_ref[...] += inner_rows(activ, down_here)

            @pl.when(first_core)
            def _():
                left_send_ref[:, :length] = pre_grad.astype(jnp.float32)

            @pl.when(jnp.logical_not(first_core))
            def _():
                left_send_ref[:, :length] = activ.astype(jnp.float32)

        @pl.when(step < steps - 1)
        def _():
            work(up_ref[...], down_ref[...], up_bias_ref[...])

        @pl.when(step == steps - 1)
        def _():
            here = step * block + lax.broadcasted_iota(jnp.int32, (block, width), 0)
            inside = here < units
            work(
                low(jnp.where(inside, up_ref[...].astype(jnp.float32), 0.0)),
                low(jnp.where(inside, down_ref[...].astype(jnp.float32), 0.0)),
                jnp.where(inside[:, :1], up_bias_ref[...], 0.0),
            )

    flat = jax.ShapeDtypeStruct((length, width), jnp.float32)
    at_row = pl.BlockSpec((1, length, width), lambda i: (row, 0, 0))
    return pl.pallas_call(
        kernel,
        grid=(steps,),
        in_specs=[scalars(), at_row]
        + [whole((length, width))] * 2
        + [whole((width,))] * 3
        + [
            pl.BlockSpec((block, width), lambda i: (i, 0)),
            pl.BlockSpec((block, 1), lambda i: (i, 0)),
            pl.BlockSpec((block, width), lambda i: (i, 0)),
            at_row,
        ]
        + [pl.BlockSpec(memory_space=pl.ANY)] * len(kept),
        out_specs=[
            whole((length, width)),
            whole((length, width)),
            pl.BlockSpec((2, block, length), lambda i: (0, i, 0)),
            pl.BlockSpec((length, width), lambda i: (row, 0)),
            whole((length, width)),
            pl.BlockSpec((block, lanes(length)), lambda i: (i, 0)),
            whole((length, width)),
        ],
        out_shape=[
            flat,
            jax.ShapeDtypeStruct((length, width), jnp.bfloat16),
            jax.ShapeDtypeStruct((2, steps * block, length), jnp.bfloat16),
            jax.ShapeDtypeStruct((hidden.shape[0] * length, width), jnp.float32),
            flat,
            jax.ShapeDtypeStruct((steps * block, lanes(length)), jnp.float32),
            flat,
        ],
        input_output_aliases={11 + number: 3 for number in range(len(kept))},
        compiler_params=limit(56),
        cost_estimate=estimate(30),
    )(
        core.reshape(1), hidden, branch, received, out_bias, gain, shift, up, up_bias, down,
        cotangent, *kept,
    )


def ff_own(core, sides, pairs, cotangent, middles, lefts, rights, counts, base):
    rows = len(pairs)
    length, columns = middles[0].shape
    streams = len(counts)
    units = sum(counts)
    firsts = [sum(counts[:number]) for number in range(streams)]
    part = base // units

    def kernel(core_ref, sides_ref, *refs):
        pair_refs = refs[:rows]
        cot_ref = refs[rows]
        middle_refs = refs[rows + 1 : 2 * rows + 1]
        left_refs = refs[2 * rows + 1 : 3 * rows + 1]
        right_refs = refs[3 * rows + 1 : 4 * rows + 1]
        out_refs = refs[4 * rows + 1 : 4 * rows + 1 + 2 * streams]
        own_ref, other_ref = refs[4 * rows + 1 + 2 * streams :]
        step = pl.program_id(0)

        @pl.when(step == 0)
        def _():
            for row in range(rows):
                other_ref[row] = low(right_refs[row][...])

        @pl.when((step == 0) & (core_ref[0] == 0))
        def _():
            for row in range(rows):
                own_ref[row] = cot_ref[row]

        @pl.when((step == 0) & (core_ref[0] != 0))
        def _():
            for row in range(rows):
                own_ref[row] = middle_refs[row][...]

        for number in range(streams):
            half = counts[number] // 2
            for keep in range(2):

                @pl.when(step == keep * streams + number)
                def _():
                    here = sides_ref[number] if keep else 1 - sides_ref[number]
                    here = pl.ds(pl.multiple_of(firsts[number] + here * half, 16), half)
                    total = product(pair_refs[0][0, here, :], own_ref[0])
                    for row in range(1, rows):
                        total = total + product(pair_refs[row][0, here, :], own_ref[row])
                    for row in range(rows):
                        left = low(left_refs[row][here, :length])
                        total = total + product(left, other_ref[row])
                    out_refs[2 * number + keep][...] = total

    shapes = [
        jax.ShapeDtypeStruct((count // 2, columns), jnp.float32)
        for count in counts
        for _ in range(2)
    ]
    return pl.pallas_call(
        kernel,
        grid_spec=pltpu.PrefetchScalarGridSpec(
            num_scalar_prefetch=2,
            grid=(2 * streams,),
            in_specs=[
                pl.BlockSpec((1, units, length), lambda step, core_ref, _: (core_ref[0], part, 0))
            ]
            * rows
            + [whole(cotangent.shape)]
            + [whole((length, columns))] * rows
            + [pl.BlockSpec((units, lanes(length)), lambda step, core_ref, _: (part, 0))] * rows
            + [whole((length, columns))] * rows,
            out_specs=[whole(shape.shape) for shape in shapes],
            scratch_shapes=[pltpu.VMEM((rows, length, columns), jnp.bfloat16)] * 2,
        ),
        out_shape=shapes,
        compiler_params=limit(56),
        cost_estimate=estimate(4),
    )(core.reshape(1), sides, *pairs, cotangent, *middles, *lefts, *rights)


def attention_own(core, dq, dk, dv, attended, normed, branch_grad, early, late):
    rows = len(dq)
    wide, length = dq[0].shape
    columns = normed[0].shape[1]
    piece = wide // 2

    def kernel(core_ref, *refs):
        groups = [refs[rows * number : rows * (number + 1)] for number in range(10)]
        dq_refs, dk_refs, dv_refs, attended_refs, normed_refs, branch_refs = groups[:6]
        early_normed, early_attended, late_refs, late_branch = groups[6:]
        out_ref = refs[10 * rows]
        step = pl.program_id(0)
        first_core = core_ref[0] == 0
        late_step = step >= 2

        def store(lefts, rights, other_lefts, other_rights):
            total = product(lefts[0][...], rights[0][...])
            for row in range(1, rows):
                total = total + product(lefts[row][...], rights[row][...])
            for row in range(rows):
                total = total + product(low(other_lefts[row]), low(other_rights[row]))
            out_ref[...] = total

        late_left = [
            ref[pl.ds(pl.multiple_of(step * piece, 16), piece), :length] for ref in late_refs
        ]

        @pl.when(jnp.logical_not(late_step) & first_core)
        def _():
            store(dq_refs, normed_refs, late_left, [ref[...] for ref in early_normed])

        @pl.when(late_step & first_core)
        def _():
            store(dk_refs, normed_refs, late_left, [ref[...] for ref in early_normed])

        @pl.when(jnp.logical_not(late_step) & jnp.logical_not(first_core))
        def _():
            store(dv_refs, normed_refs, late_left, [ref[...] for ref in early_normed])

        @pl.when(late_step & jnp.logical_not(first_core))
        def _():
            store(
                attended_refs,
                branch_refs,
                [ref[:, :length] for ref in early_attended],
                [ref[...] for ref in late_branch],
            )

    def first_half(wide_here):
        return pl.BlockSpec((piece, wide_here), lambda step, core_ref: (jnp.minimum(step, 1), 0))

    def second_half(wide_here):
        return pl.BlockSpec(
            (piece, wide_here), lambda step, core_ref: (jnp.maximum(step - 2, 0), 0)
        )

    wholes = [whole((length, columns))] * rows
    return pl.pallas_call(
        kernel,
        grid_spec=pltpu.PrefetchScalarGridSpec(
            num_scalar_prefetch=1,
            grid=(4,),
            in_specs=([first_half(length)] * rows + [second_half(length)] * rows) * 2
            + wholes * 2
            + wholes
            + [second_half(lanes(length))] * rows
            + [whole(late[0][0].shape)] * rows
            + wholes,
            out_specs=pl.BlockSpec((piece, columns), lambda step, core_ref: (step, 0)),
        ),
        out_shape=jax.ShapeDtypeStruct((2 * wide, columns), jnp.float32),
        compiler_params=limit(56),
        cost_estimate=estimate(0.02),
    )(
        core.reshape(1), *dq, *dk, *dv, *attended, *normed, *branch_grad,
        *[member for place in range(2) for member in [part[place] for part in early]],
        *[member for place in range(2) for member in [part[place] for part in late]],
    )


def shards(
    hidden_in,
    row_layout,
    cotangent,
    pre_gain,
    pre_shift,
    query_weight,
    query_bias,
    key_weight,
    value_weight,
    value_bias,
    out_weight,
    out_bias,
    mid_gain,
    mid_shift,
    up_weight,
    up_bias,
    down_weight,
    down_bias,
):
    rows, length, width = hidden_in.shape
    tokens = rows * length
    heads_wide = query_weight.shape[1]
    hidden = up_weight.shape[1]
    side = sides()
    core = side["core"]
    order = Order()
    query_turned = query_weight.T
    key_turned = key_weight.T
    value_turned = value_weight.T
    up_turned = up_weight.T

    forward = [
        order.run(
            lambda ready: attention_forward(
                row, row_layout, ready, pre_gain, pre_shift, query_turned, query_bias, key_turned,
                value_turned, value_bias, out_weight,
            ),
            hidden_in,
        )
        for row in range(rows)
    ]

    up_column = up_bias.reshape(-1, 1)
    middle = []
    early = []
    for row in range(rows):
        if row > 0:
            with jax.named_scope("early_core_move_" + str(row - 1)):
                early.append(order.settle([swap(forward[row - 1].value[n], "core") for n in (6, 7)]))
        with jax.named_scope("branch_move_" + str(row)):
            received = swap_tensor(forward[row].value[5])
        middle.append(
            order.run(
                lambda ready: feed_forward(
                    row, core, hidden_in, ready, received, out_bias, mid_gain, mid_shift,
                    up_turned, up_column, down_weight, cotangent,
                    None if row == 0 else middle[row - 1].value[3],
                ),
                forward[row].value[5],
            )
        )
    with jax.named_scope("early_core_move_" + str(rows - 1)):
        early.append(order.settle([swap(forward[rows - 1].value[n], "core") for n in (6, 7)]))
    normed = [forward[row].value[0] for row in range(rows)]
    attended = [forward[row].value[4] for row in range(rows)]
    resid = [middle[row].value[0] for row in range(rows)]
    middles = [middle[row].value[1] for row in range(rows)]
    backward = []

    def back(row, received):
        _, q, k, v = forward[row].value[:4]
        backward.append(
            order.run(
                lambda ready: attention_backward(
                    row, core, row_layout, ready, received, resid[row], cotangent, mid_gain,
                    q, k, v, out_weight,
                ),
                middle[rows - 1].value[3],
            )
        )

    pairs = [middle[row].value[2] for row in range(rows)]
    ff_rows = (576, 576, 576, 576)
    ff_streams = [Stream("ff" + str(n), order, ORDERS[n], side) for n in range(4)]

    def ff_step(extra=None):
        moved = [stream.moved() for stream in ff_streams]
        received = lax.optimization_barrier(moved + ([] if extra is None else [extra]))
        for stream, part in zip(ff_streams, received):
            stream.step(part)
        return received[-1]

    lefts, rights = [], []

    def ff_core_move(row):
        with jax.named_scope("ff_core_move_" + str(row)):
            lefts.append(swap(middle[row].value[5], "core"))
            rights.append(swap(middle[row].value[6], "core"))

    ff_core_move(0)
    lefts[0] = order.settle(lefts[0])
    rights[0] = order.settle(rights[0])
    ff_core_move(1)
    ff_sides = jnp.stack([side[stream.pairs[0]] for stream in ff_streams])

    halves = order.run(
        lambda ready: ff_own(
            core, ff_sides, [pairs[0], ready], cotangent, middles, lefts, rights, ff_rows, 0
        ),
        pairs[1],
    )
    for n, stream in enumerate(ff_streams):
        stream.begin(*halves.value[2 * n : 2 * n + 2])
    with jax.named_scope("mid_move"):
        mid_received = swap_tensor(middle[rows - 1].value[3])
    back(0, mid_received)
    back(1, mid_received)

    dq, dk, dv = ([backward[row].value[place] for row in range(rows)] for place in (3, 4, 5))
    branch_grad = [backward[row].value[1] for row in range(rows)]
    output = []

    def output_move(row):
        with jax.named_scope("output_move_" + str(row)):
            return swap_tensor(middle[row].value[4])

    def output_row(row, received):
        output.append(
            order.run(
                lambda ready: low(resid[row] + (ready + received) + down_bias),
                middle[row].value[4],
            )
        )

    def normed_move(row):
        with jax.named_scope("normed_move_" + str(row)):
            return swap_tensor(normed_part[row].value)

    output_received = ff_step(output_move(0))
    late = []
    for row in range(rows):
        with jax.named_scope("late_core_move_" + str(row)):
            late.append(order.settle([swap(backward[row].value[n], "core") for n in (6, 7)]))
    at_own = order.run(
        lambda ready: attention_own(
            core, [dq[0], ready], dk, dv, attended, normed, branch_grad, early, late
        ),
        dq[1],
    )
    with jax.named_scope("at_scatter"):
        at_block = lax.psum_scatter(
            at_own.value, "dp", axis_index_groups=PLANES, scatter_dimension=0, tiled=True
        )
    normed_part = [
        order.run(
            lambda ready: inner_rows(ready, query_turned)
            + inner_rows(dk[row], key_turned)
            + inner_rows(dv[row], value_turned),
            dq[row],
        )
        for row in range(rows)
    ]
    ff_step()
    output_row(0, output_received)
    normed_received = [ff_step(normed_move(0))]
    normed_received.append(ff_step(normed_move(1)))
    normed_grad = order.run(
        lambda ready: jnp.concatenate(
            [ready + normed_received[0], normed_part[1].value + normed_received[1]], 0
        ),
        normed_part[0].value,
    )
    normed_grad.value, sum_dq, sum_dv, sum_pairs, sum_cotangent = lax.optimization_barrier(
        (normed_grad.value, dq, dv, pairs, cotangent)
    )

    pre_normal, pre_factor = normalized(hidden_in.reshape(tokens, width).astype(jnp.float32))
    pre_gain_grad = jnp.sum(normed_grad.value * pre_normal, axis=0)
    pre_shift_grad = jnp.sum(normed_grad.value, axis=0)
    resid_grad = jnp.concatenate([backward[row].value[0] for row in range(rows)], 0)
    input_grad = resid_grad + norm_back(normed_grad.value, pre_normal, pre_factor, pre_gain)
    terms = sum(backward[row].value[2] for row in range(rows))

    def token_sum(members):
        return sum(jnp.sum(member.astype(jnp.float32), axis=1) for member in members)

    small = jnp.concatenate(
        [
            pre_gain_grad,
            pre_shift_grad,
            terms[2],
            terms[0],
            terms[1],
            jnp.sum(sum_cotangent.astype(jnp.float32), axis=(0, 1)),
            token_sum(sum_dq),
            token_sum(sum_dv),
            token_sum([pair[1, :hidden] for pair in sum_pairs]),
            jnp.zeros((2 * width - hidden,), jnp.float32),
        ]
    ).reshape(9, width)
    small = order.run(lambda ready: ready, small)

    def small_move(pair):
        with jax.named_scope("small_move_" + pair):
            return swap(small.value, pair)

    def small_add(received):
        return order.run(lambda ready: ready + received, small.value)

    small = small_add(ff_step(small_move("z")))
    small = small_add(ff_step(small_move("xa")))
    small = small_add(ff_step(small_move("ya")))
    at_block = order.run(lambda ready: ready + 0.0, at_block)
    with jax.named_scope("at_z_move"):
        received = swap(at_block.value, "z")
    received = ff_step(received)
    halves = [stream.halves() for stream in ff_streams]
    at_block = order.run(lambda ready: ready + received, at_block.value)
    with jax.named_scope("at_gather"):
        at_whole = lax.all_gather(
            at_block.value, "dp", axis_index_groups=PLANES, axis=0, tiled=True
        )
    others = order.settle([other for _, other in halves] + [output_move(1)])
    output_row(1, others.pop())
    far = []
    for number, other in enumerate(others):
        with jax.named_scope("ff_core_other_" + str(number)):
            far.append((swap(halves[number][0], "core"), swap(other, "core")))
    down_up = None
    for n in range(4):
        down_up = pick_halves(
            core, ff_sides[n : n + 1], (halves[n][0], others[n], *far[n]), hidden,
            sum(ff_rows[:n]), down_up,
        )
        first_down, small.value = lax.optimization_barrier((down_up[0], small.value))
        down_up = (first_down, down_up[1])
        if n < 3:
            small = small_add(small_move(("xb", "yb", "core")[n]))
    down_grad, up_grad = down_up
    input_low, small.value, at_whole, down_grad = lax.optimization_barrier(
        (low(input_grad), small.value, at_whole, down_grad)
    )
    with jax.named_scope("at_core_back"):
        received = swap(at_whole, "core")
    query_weight_grad, value_weight_grad = pick_rows(
        core, at_whole, received, heads_wide, 192, 0, 0, heads_wide
    )
    key_weight_grad, out_grad = pick_rows(
        core, at_whole, received, heads_wide, 192, heads_wide, 0, heads_wide
    )
    small = small.value
    return (
        jnp.stack([part.value for part in output]),
        input_low.reshape(hidden_in.shape),
        small[0],
        small[1],
        query_weight_grad.T,
        small[6, :heads_wide],
        key_weight_grad.T,
        value_weight_grad.T,
        small[6, heads_wide:],
        out_grad,
        small[2],
        small[3],
        small[4],
        up_grad.T,
        small[7:].reshape(-1)[:hidden],
        down_grad,
        small[5],
    )


def solution(mesh):
    placed = (
        P("dp", None, None),
        P("dp", None),
        P("dp", None, None),
        P(),
        P(),
        P(None, "tensor"),
        P("tensor"),
        P(None, "tensor"),
        P(None, "tensor"),
        P("tensor"),
        P("tensor", None),
        P(),
        P(),
        P(),
        P(None, "tensor"),
        P("tensor"),
        P("tensor", None),
        P(),
    )
    return jax.shard_map(
        shards,
        mesh=mesh,
        in_specs=placed,
        out_specs=(
            P("dp", None, None),
            P("dp", None, None),
            P(),
            P(),
            P(None, "tensor"),
            P("tensor"),
            P(None, "tensor"),
            P(None, "tensor"),
            P("tensor"),
            P("tensor", None),
            P(),
            P(),
            P(),
            P(None, "tensor"),
            P("tensor"),
            P("tensor", None),
            P(),
        ),
        check_vma=False,
    )
```

```python
import jax
import jax.numpy as jnp
from jax import lax
from jax.experimental import pallas as pl
from jax.experimental.pallas import tpu as pltpu
from jax.sharding import PartitionSpec as P

HEAD = 72
norm_epsilon = 1e-06


def partner_pairs(move):
    pairs = []
    for place in range(64):
        z_hi, x, y, core = place >> 5, (place >> 3) & 3, (place >> 1) & 3, place & 1
        z_hi, x, y, core = move(z_hi, x, y, core)
        pairs.append((place, ((z_hi * 4 + x) * 4 + y) * 2 + core))
    return pairs


PAIRS = {
    "core": partner_pairs(lambda z, x, y, c: (z, x, y, 1 - c)),
    "xa": partner_pairs(lambda z, x, y, c: (z, x ^ 1, y, c)),
    "xb": partner_pairs(lambda z, x, y, c: (z, x ^ 3, y, c)),
    "ya": partner_pairs(lambda z, x, y, c: (z, x, y ^ 1, c)),
    "yb": partner_pairs(lambda z, x, y, c: (z, x, y ^ 3, c)),
    "z": partner_pairs(lambda z, x, y, c: (1 - z, x, y, c)),
}
PLANES = [
    [((z_hi * 4 + x) * 4 + y) * 2 + core for x in range(4) for y in range(4)]
    for z_hi in range(2)
    for core in range(2)
]
ORDERS = (
    ("xa", "ya", "xb", "yb"),
    ("ya", "xb", "yb", "xa"),
    ("xb", "yb", "xa", "ya"),
    ("yb", "xa", "ya", "xb"),
)


def sides():
    place = lax.axis_index("dp")
    x = (place >> 3) & 3
    y = (place >> 1) & 3
    return {
        "core": place & 1,
        "xa": (x ^ (x >> 1)) & 1,
        "xb": x >> 1,
        "ya": (y ^ (y >> 1)) & 1,
        "yb": y >> 1,
    }


def swap(values, pair):
    return lax.ppermute(values, "dp", PAIRS[pair])


def swap_tensor(values):
    return lax.ppermute(values, "tensor", [(0, 1), (1, 0)])


class Cell:
    def __init__(self, value):
        self.value = value


class Order:
    def __init__(self):
        self.last = None

    def run(self, operation, ready):
        if self.last is not None:
            self.last.value, ready = lax.optimization_barrier((self.last.value, ready))
        self.last = Cell(operation(ready))
        return self.last

    def settle(self, value):
        self.last.value, value = lax.optimization_barrier((self.last.value, value))
        return value


def half_of(values, side):
    count = values.shape[0] // 2
    return lax.dynamic_slice_in_dim(values, side * count, count, 0)


def row_half_of(values, side):
    count = values.shape[1] // 2
    return jnp.where(side == 0, values[:, :count], values[:, count:])


def joined(own, received, side, axis):
    return jnp.where(
        side == 0,
        jnp.concatenate([own, received], axis),
        jnp.concatenate([received, own], axis),
    )


class Stream:
    def __init__(self, name, order, pairs, side):
        self.name = name
        self.order = order
        self.pairs = pairs
        self.side = side
        self.stage = 0
        self.keep = None
        self.sent = None

    def begin(self, send, keep):
        four = (4, send.shape[0] // 4, send.shape[1])
        self.sent = Cell(send.reshape(four))
        self.order.last = self.sent
        self.keep = keep.reshape(four)
        self.stage = 1

    def moved(self):
        pairs = self.pairs
        stage = self.stage
        with jax.named_scope(self.name + "_move_" + str(stage)):
            if stage <= 4:
                return swap(self.sent.value, pairs[stage - 1])
            if stage == 5:
                return swap(self.sent.value, "z")
            return swap(self.sent.value, pairs[9 - stage])

    def step(self, received):
        pairs = self.pairs
        stage = self.stage
        self.stage += 1
        keep = self.keep
        with jax.named_scope(self.name + "_sum_" + str(stage)):
            if stage <= 3:
                take = half_of if stage < 3 else row_half_of
                side = self.side[pairs[stage]]
                self.keep = take(keep, side) + take(received, side)
                self.sent = self.order.run(
                    lambda ready: take(ready, 1 - side) + take(received, 1 - side), keep
                )
            elif stage == 4:
                self.sent = self.order.run(lambda ready: ready + received, keep)
            elif stage == 5:
                self.sent = self.order.run(lambda ready: ready + received, self.sent.value)
            else:
                axis = 1 if stage == 6 else 0
                pair = pairs[9 - stage]
                self.sent = self.order.run(
                    lambda ready: joined(ready, received, self.side[pair], axis), self.sent.value
                )

    def halves(self):
        here = self.sent.value
        flat = (-1, here.shape[2])
        return here.reshape(flat), self.moved().reshape(flat)


def pick_rows(core, own, other, rows, block, skipped, first, total, kept=()):
    columns = own.shape[1]
    before, start = skipped // block, first // block

    def kernel(core_ref, own_ref, other_ref, *refs):
        first_ref, second_ref = refs[-2:]

        @pl.when(core_ref[0] == 0)
        def _():
            first_ref[...] = own_ref[...]
            second_ref[...] = other_ref[...]

        @pl.when(core_ref[0] != 0)
        def _():
            first_ref[...] = other_ref[...]
            second_ref[...] = own_ref[...]

    shape = jax.ShapeDtypeStruct((total, columns), jnp.float32)
    in_spec = pl.BlockSpec((block, columns), lambda i, core_ref: (before + i, 0))
    out_spec = pl.BlockSpec((block, columns), lambda i, core_ref: (start + i, 0))
    return pl.pallas_call(
        kernel,
        grid_spec=pltpu.PrefetchScalarGridSpec(
            num_scalar_prefetch=1,
            grid=(-(-rows // block),),
            in_specs=[in_spec, in_spec] + [pl.BlockSpec(memory_space=pl.ANY)] * len(kept),
            out_specs=(out_spec, out_spec),
        ),
        out_shape=(shape, shape),
        input_output_aliases={3 + number: number for number in range(len(kept))},
        compiler_params=limit(20),
        cost_estimate=estimate(8),
    )(core.reshape(1), own, other, *kept)


def pick_halves(core, sides, pieces, rows, first, before):
    half, columns = pieces[0].shape
    block = half // 2
    start = first // block

    def kernel(core_ref, sides_ref, *refs):
        first_ref, second_ref = refs[-2:]
        here = (pl.program_id(0) // 2) == sides_ref[0]
        for other in range(2):
            own_ref, far_ref = refs[other], refs[2 + other]
            chosen = here if other == 0 else jnp.logical_not(here)

            @pl.when(chosen & (core_ref[0] == 0))
            def _():
                first_ref[...] = own_ref[...]
                second_ref[...] = far_ref[...]

            @pl.when(chosen & (core_ref[0] != 0))
            def _():
                first_ref[...] = far_ref[...]
                second_ref[...] = own_ref[...]

    def place(other):
        def index(i, core_ref, sides_ref):
            side = sides_ref[0] if other == 0 else 1 - sides_ref[0]
            return (jnp.clip(i - side * 2, 0, 1), 0)

        return pl.BlockSpec((block, columns), index)

    shape = jax.ShapeDtypeStruct((rows, columns), jnp.float32)
    out_spec = pl.BlockSpec((block, columns), lambda i, core_ref, sides_ref: (start + i, 0))
    steps = min(4, -(-(rows - first) // block))
    kept = [] if before is None else list(before)
    return pl.pallas_call(
        kernel,
        grid_spec=pltpu.PrefetchScalarGridSpec(
            num_scalar_prefetch=2,
            grid=(steps,),
            in_specs=[place(other) for other in (0, 1, 0, 1)]
            + [pl.BlockSpec(memory_space=pl.ANY)] * len(kept),
            out_specs=(out_spec, out_spec),
        ),
        out_shape=(shape, shape),
        input_output_aliases={6 + number: number for number in range(len(kept))},
        compiler_params=limit(20),
        cost_estimate=estimate(4),
    )(core.reshape(1), sides, *pieces, *kept)


GELU_SCALE = (2.0 / 3.141592653589793) ** 0.5


def across(left, right):
    return lax.dot_general(
        left, right, (((1,), (1,)), ((), ())), preferred_element_type=jnp.float32
    )


def inner_rows(left, right):
    return lax.dot_general(
        left, right, (((0,), (0,)), ((), ())), preferred_element_type=jnp.float32
    )


def product(left, right):
    return jnp.dot(left, right, preferred_element_type=jnp.float32)


def normalized(values):
    center = values - jnp.mean(values, axis=-1, keepdims=True)
    spread = jnp.mean(center * center, axis=-1, keepdims=True)
    factor = lax.rsqrt(spread + norm_epsilon)
    return center * factor, factor


def norm_back(grad, normal, factor, gain):
    scaled = grad * gain
    mean_scaled = jnp.mean(scaled, axis=-1, keepdims=True)
    mean_normal = jnp.mean(scaled * normal, axis=-1, keepdims=True)
    return factor * (scaled - mean_scaled - normal * mean_normal)


def same_segment(layout_ref, row, length):
    def segment(axis):
        places = lax.broadcasted_iota(jnp.int32, (length, length), axis)
        total = jnp.zeros((length, length), jnp.int32)
        bound = 0
        for picture in range(3):
            bound = bound + layout_ref[row, picture]
            total = total + (places >= bound).astype(jnp.int32)
        return total

    return segment(0) == segment(1)


def head_probs(query, key, same):
    scores = inner_rows(query, key) * (HEAD ** (-0.5))
    scores = jnp.where(same, scores, -1000000000.0)
    exponent = jnp.exp(scores - jnp.max(scores, axis=-1, keepdims=True))
    return exponent / jnp.sum(exponent, axis=-1, keepdims=True)


def as_column(vector):
    return jnp.broadcast_to(vector[None, :], (8, vector.shape[0])).T[:, 0:1]


def lanes(count):
    return -(-count // 128) * 128


def whole(shape):
    return pl.BlockSpec(shape, lambda *_: (0,) * len(shape))


def scalars():
    return pl.BlockSpec(memory_space=pltpu.SMEM)


def estimate(microseconds):
    return pl.CostEstimate(
        flops=int(microseconds * 1.15e9), bytes_accessed=1024, transcendentals=0
    )


def limit(mebibytes):
    return pltpu.CompilerParams(vmem_limit_bytes=mebibytes * 1024 * 1024)


def low(values):
    return values.astype(jnp.bfloat16)


def attention_forward(row, layout, hidden, gain, shift, wq, bq, wk, wv, bv, wo):
    _, length, width = hidden.shape
    wide = wq.shape[0]

    def kernel(
        layout_ref, hidden_ref, gain_ref, shift_ref, wq_ref, bq_ref, wk_ref, wv_ref, bv_ref,
        wo_ref, normed_ref, q_ref, k_ref, v_ref, att_ref, branch_ref, normed_send_ref, att_send_ref,
    ):
        normal, _ = normalized(hidden_ref[0].astype(jnp.float32))
        normed = low(normal * gain_ref[...][None, :] + shift_ref[...][None, :])
        normed_ref[...] = normed
        normed_send_ref[...] = normed.astype(jnp.float32)
        queries = low(across(wq_ref[...], normed) + as_column(bq_ref[...]))
        keys = low(across(wk_ref[...], normed))
        values = low(across(wv_ref[...], normed) + as_column(bv_ref[...]))
        q_ref[...] = queries
        k_ref[...] = keys
        v_ref[...] = values
        queries, keys, values = (part.astype(jnp.float32) for part in (queries, keys, values))
        same = same_segment(layout_ref, row, length)
        parts = []
        for head in range(wide // HEAD):
            rows = slice(head * HEAD, (head + 1) * HEAD)
            probs = head_probs(low(queries[rows]), low(keys[rows]), same)
            parts.append(across(low(values[rows]), low(probs)))
        attended = low(jnp.concatenate(parts, 0))
        att_ref[...] = attended
        att_send_ref[:, :length] = attended.astype(jnp.float32)
        att_send_ref[:, length:] = jnp.zeros((wide, lanes(length) - length), jnp.float32)
        branch_ref[...] = inner_rows(attended, wo_ref[...])

    turned = jax.ShapeDtypeStruct((wide, length), jnp.bfloat16)
    return pl.pallas_call(
        kernel,
        grid=(1,),
        in_specs=[
            scalars(),
            pl.BlockSpec((1, length, width), lambda i: (row, 0, 0)),
            whole((width,)),
            whole((width,)),
            whole((wide, width)),
            whole((wide,)),
            whole((wide, width)),
            whole((wide, width)),
            whole((wide,)),
            whole((wide, width)),
        ],
        out_specs=[whole((length, width))]
        + [whole((wide, length))] * 4
        + [whole((length, width))] * 2
        + [whole((wide, lanes(length)))],
        out_shape=[
            jax.ShapeDtypeStruct((length, width), jnp.bfloat16),
            turned,
            turned,
            turned,
            turned,
            jax.ShapeDtypeStruct((length, width), jnp.float32),
            jax.ShapeDtypeStruct((length, width), jnp.float32),
            jax.ShapeDtypeStruct((wide, lanes(length)), jnp.float32),
        ],
        compiler_params=limit(56),
        cost_estimate=estimate(20),
    )(layout, hidden, gain, shift, wq, bq, wk, wv, bv, wo)


def attention_backward(row, core, layout, part, received, resid, cotangent, gain, q, k, v, wo):
    _, length, width = cotangent.shape
    wide = wo.shape[0]

    def kernel(
        core_ref, layout_ref, part_ref, received_ref, resid_ref, cot_ref, gain_ref, q_ref, k_ref, v_ref,
        wo_ref, resid_grad_ref, branch_grad_ref, terms_ref, dq_ref, dk_ref, dv_ref, send_ref,
        branch_send_ref,
    ):
        mid_grad = part_ref[...] + received_ref[...]
        normal, factor = normalized(resid_ref[...])
        terms_ref[0:1, :] = jnp.sum(mid_grad * normal, axis=0, keepdims=True)
        terms_ref[1:2, :] = jnp.sum(mid_grad, axis=0, keepdims=True)
        resid_grad = cot_ref[0].astype(jnp.float32) + norm_back(
            mid_grad, normal, factor, gain_ref[...][None, :]
        )
        resid_grad_ref[...] = resid_grad
        branch_grad = low(resid_grad)
        branch_grad_ref[...] = branch_grad
        branch_send_ref[...] = branch_grad.astype(jnp.float32)
        terms_ref[2:3, :] = jnp.sum(branch_grad.astype(jnp.float32), axis=0, keepdims=True)
        terms_ref[3:8, :] = jnp.zeros((5, width), jnp.float32)
        back = low(across(wo_ref[...], branch_grad)).astype(jnp.float32)
        same = same_segment(layout_ref, row, length)
        queries, keys, values = (
            ref[...].astype(jnp.float32) for ref in (q_ref, k_ref, v_ref)
        )
        dq, dk, dv = [], [], []
        for head in range(wide // HEAD):
            rows = slice(head * HEAD, (head + 1) * HEAD)
            query, key, value, grad = (
                low(member[rows]) for member in (queries, keys, values, back)
            )
            probs = head_probs(query, key, same)
            dv.append(product(grad, low(probs)))
            prob_grad = inner_rows(grad, value)
            inside = prob_grad - jnp.sum(prob_grad * probs, axis=-1, keepdims=True)
            score_grad = low(probs * inside)
            dq.append(across(key, score_grad) * (HEAD ** (-0.5)))
            dk.append(product(query, score_grad) * (HEAD ** (-0.5)))
        dq, dk, dv = (low(jnp.concatenate(parts, 0)) for parts in (dq, dk, dv))
        dq_ref[...] = dq
        dk_ref[...] = dk
        dv_ref[...] = dv
        send_ref[: 2 * wide, length:] = jnp.zeros((2 * wide, lanes(length) - length), jnp.float32)
        send_ref[wide : 2 * wide, :length] = dk.astype(jnp.float32)

        @pl.when(core_ref[0] == 0)
        def _():
            send_ref[:wide, :length] = dv.astype(jnp.float32)

        @pl.when(core_ref[0] != 0)
        def _():
            send_ref[:wide, :length] = dq.astype(jnp.float32)

    turned = jax.ShapeDtypeStruct((wide, length), jnp.bfloat16)
    return pl.pallas_call(
        kernel,
        grid=(1,),
        in_specs=[scalars(), scalars()]
        + [pl.BlockSpec((length, width), lambda i: (row, 0))] * 2
        + [whole((length, width))]
        + [pl.BlockSpec((1, length, width), lambda i: (row, 0, 0)), whole((width,))]
        + [whole((wide, length))] * 3
        + [whole((wide, width))],
        out_specs=[whole((length, width)), whole((length, width)), whole((8, width))]
        + [whole((wide, length))] * 3
        + [whole((2 * wide, lanes(length))), whole((length, width))],
        out_shape=[
            jax.ShapeDtypeStruct((length, width), jnp.float32),
            jax.ShapeDtypeStruct((length, width), jnp.bfloat16),
            jax.ShapeDtypeStruct((8, width), jnp.float32),
            turned,
            turned,
            turned,
            jax.ShapeDtypeStruct((2 * wide, lanes(length)), jnp.float32),
            jax.ShapeDtypeStruct((length, width), jnp.float32),
        ],
        compiler_params=limit(56),
        cost_estimate=estimate(0.02),
    )(core.reshape(1), layout, part, received, resid, cotangent, gain, q, k, v, wo)


def feed_forward(
    row, core, hidden, branch, received, out_bias, gain, shift, up, up_bias, down, cotangent,
    mid_parts=None,
):
    _, length, width = hidden.shape
    units = up.shape[0]
    kept = [] if mid_parts is None else [mid_parts]
    block = 768
    steps = -(-units // block)

    def kernel(
        core_ref, hidden_ref, branch_ref, received_ref, out_bias_ref, gain_ref, shift_ref, up_ref,
        up_bias_ref, down_ref, cot_ref, *refs,
    ):
        resid_ref, middle_ref, pair_ref, mid_part_ref, out_part_ref = refs[-7:-2]
        left_send_ref, right_send_ref = refs[-2:]
        step = pl.program_id(0)
        first_core = core_ref[0] == 0

        @pl.when(step == 0)
        def _():
            resid = hidden_ref[0].astype(jnp.float32) + (
                (branch_ref[...] + received_ref[...]) + out_bias_ref[...][None, :]
            )
            resid_ref[...] = resid
            normal, _ = normalized(resid)
            middle = low(normal * gain_ref[...][None, :] + shift_ref[...][None, :])
            middle_ref[...] = middle
            mid_part_ref[...] = jnp.zeros((length, width), jnp.float32)
            out_part_ref[...] = jnp.zeros((length, width), jnp.float32)

            @pl.when(first_core)
            def _():
                right_send_ref[...] = middle.astype(jnp.float32)

            @pl.when(jnp.logical_not(first_core))
            def _():
                right_send_ref[...] = cot_ref[0].astype(jnp.float32)

        def work(up_here, down_here, up_bias_here):
            act = across(up_here, middle_ref[...]) + up_bias_here
            act_grad = across(down_here, cot_ref[0])
            curve = jnp.tanh(GELU_SCALE * (act + 0.044715 * (act * act * act)))
            activ = low(0.5 * act * (1.0 + curve))
            slope = 0.5 * (1.0 + curve) + 0.5 * act * (1.0 - curve * curve) * (
                GELU_SCALE * (1.0 + 3.0 * 0.044715 * (act * act))
            )
            pre_grad = low(act_grad * slope)
            pair_ref[0] = activ
            pair_ref[1] = pre_grad
            left_send_ref[:, length:] = jnp.zeros((block, lanes(length) - length), jnp.float32)
            mid_part_ref[...] += inner_rows(pre_grad, up_here)
            out_part_ref[...] += inner_rows(activ, down_here)

            @pl.when(first_core)
            def _():
                left_send_ref[:, :length] = pre_grad.astype(jnp.float32)

            @pl.when(jnp.logical_not(first_core))
            def _():
                left_send_ref[:, :length] = activ.astype(jnp.float32)

        @pl.when(step < steps - 1)
        def _():
            work(up_ref[...], down_ref[...], up_bias_ref[...])

        @pl.when(step == steps - 1)
        def _():
            here = step * block + lax.broadcasted_iota(jnp.int32, (block, width), 0)
            inside = here < units
            work(
                low(jnp.where(inside, up_ref[...].astype(jnp.float32), 0.0)),
                low(jnp.where(inside, down_ref[...].astype(jnp.float32), 0.0)),
                jnp.where(inside[:, :1], up_bias_ref[...], 0.0),
            )

    flat = jax.ShapeDtypeStruct((length, width), jnp.float32)
    at_row = pl.BlockSpec((1, length, width), lambda i: (row, 0, 0))
    return pl.pallas_call(
        kernel,
        grid=(steps,),
        in_specs=[scalars(), at_row]
        + [whole((length, width))] * 2
        + [whole((width,))] * 3
        + [
            pl.BlockSpec((block, width), lambda i: (i, 0)),
            pl.BlockSpec((block, 1), lambda i: (i, 0)),
            pl.BlockSpec((block, width), lambda i: (i, 0)),
            at_row,
        ]
        + [pl.BlockSpec(memory_space=pl.ANY)] * len(kept),
        out_specs=[
            whole((length, width)),
            whole((length, width)),
            pl.BlockSpec((2, block, length), lambda i: (0, i, 0)),
            pl.BlockSpec((length, width), lambda i: (row, 0)),
            whole((length, width)),
            pl.BlockSpec((block, lanes(length)), lambda i: (i, 0)),
            whole((length, width)),
        ],
        out_shape=[
            flat,
            jax.ShapeDtypeStruct((length, width), jnp.bfloat16),
            jax.ShapeDtypeStruct((2, steps * block, length), jnp.bfloat16),
            jax.ShapeDtypeStruct((hidden.shape[0] * length, width), jnp.float32),
            flat,
            jax.ShapeDtypeStruct((steps * block, lanes(length)), jnp.float32),
            flat,
        ],
        input_output_aliases={11 + number: 3 for number in range(len(kept))},
        compiler_params=limit(56),
        cost_estimate=estimate(30),
    )(
        core.reshape(1), hidden, branch, received, out_bias, gain, shift, up, up_bias, down,
        cotangent, *kept,
    )


def ff_own(core, sides, pairs, cotangent, middles, lefts, rights, counts, base):
    rows = len(pairs)
    length, columns = middles[0].shape
    streams = len(counts)
    units = sum(counts)
    firsts = [sum(counts[:number]) for number in range(streams)]
    part = base // units

    def kernel(core_ref, sides_ref, *refs):
        pair_refs = refs[:rows]
        cot_ref = refs[rows]
        middle_refs = refs[rows + 1 : 2 * rows + 1]
        left_refs = refs[2 * rows + 1 : 3 * rows + 1]
        right_refs = refs[3 * rows + 1 : 4 * rows + 1]
        out_refs = refs[4 * rows + 1 : 4 * rows + 1 + 2 * streams]
        own_ref, other_ref = refs[4 * rows + 1 + 2 * streams :]
        step = pl.program_id(0)

        @pl.when(step == 0)
        def _():
            for row in range(rows):
                other_ref[row] = low(right_refs[row][...])

        @pl.when((step == 0) & (core_ref[0] == 0))
        def _():
            for row in range(rows):
                own_ref[row] = cot_ref[row]

        @pl.when((step == 0) & (core_ref[0] != 0))
        def _():
            for row in range(rows):
                own_ref[row] = middle_refs[row][...]

        for number in range(streams):
            half = counts[number] // 2
            for keep in range(2):

                @pl.when(step == keep * streams + number)
                def _():
                    here = sides_ref[number] if keep else 1 - sides_ref[number]
                    here = pl.ds(pl.multiple_of(firsts[number] + here * half, 16), half)
                    total = product(pair_refs[0][0, here, :], own_ref[0])
                    for row in range(1, rows):
                        total = total + product(pair_refs[row][0, here, :], own_ref[row])
                    for row in range(rows):
                        left = low(left_refs[row][here, :length])
                        total = total + product(left, other_ref[row])
                    out_refs[2 * number + keep][...] = total

    shapes = [
        jax.ShapeDtypeStruct((count // 2, columns), jnp.float32)
        for count in counts
        for _ in range(2)
    ]
    return pl.pallas_call(
        kernel,
        grid_spec=pltpu.PrefetchScalarGridSpec(
            num_scalar_prefetch=2,
            grid=(2 * streams,),
            in_specs=[
                pl.BlockSpec((1, units, length), lambda step, core_ref, _: (core_ref[0], part, 0))
            ]
            * rows
            + [whole(cotangent.shape)]
            + [whole((length, columns))] * rows
            + [pl.BlockSpec((units, lanes(length)), lambda step, core_ref, _: (part, 0))] * rows
            + [whole((length, columns))] * rows,
            out_specs=[whole(shape.shape) for shape in shapes],
            scratch_shapes=[pltpu.VMEM((rows, length, columns), jnp.bfloat16)] * 2,
        ),
        out_shape=shapes,
        compiler_params=limit(56),
        cost_estimate=estimate(4),
    )(core.reshape(1), sides, *pairs, cotangent, *middles, *lefts, *rights)


def attention_own(core, dq, dk, dv, attended, normed, branch_grad, early, late):
    rows = len(dq)
    wide, length = dq[0].shape
    columns = normed[0].shape[1]
    piece = wide // 2

    def kernel(core_ref, *refs):
        groups = [refs[rows * number : rows * (number + 1)] for number in range(10)]
        dq_refs, dk_refs, dv_refs, attended_refs, normed_refs, branch_refs = groups[:6]
        early_normed, early_attended, late_refs, late_branch = groups[6:]
        out_ref = refs[10 * rows]
        step = pl.program_id(0)
        first_core = core_ref[0] == 0
        late_step = step >= 2

        def store(lefts, rights, other_lefts, other_rights):
            total = product(lefts[0][...], rights[0][...])
            for row in range(1, rows):
                total = total + product(lefts[row][...], rights[row][...])
            for row in range(rows):
                total = total + product(low(other_lefts[row]), low(other_rights[row]))
            out_ref[...] = total

        late_left = [
            ref[pl.ds(pl.multiple_of(step * piece, 16), piece), :length] for ref in late_refs
        ]

        @pl.when(jnp.logical_not(late_step) & first_core)
        def _():
            store(dq_refs, normed_refs, late_left, [ref[...] for ref in early_normed])

        @pl.when(late_step & first_core)
        def _():
            store(dk_refs, normed_refs, late_left, [ref[...] for ref in early_normed])

        @pl.when(jnp.logical_not(late_step) & jnp.logical_not(first_core))
        def _():
            store(dv_refs, normed_refs, late_left, [ref[...] for ref in early_normed])

        @pl.when(late_step & jnp.logical_not(first_core))
        def _():
            store(
                attended_refs,
                branch_refs,
                [ref[:, :length] for ref in early_attended],
                [ref[...] for ref in late_branch],
            )

    def first_half(wide_here):
        return pl.BlockSpec((piece, wide_here), lambda step, core_ref: (jnp.minimum(step, 1), 0))

    def second_half(wide_here):
        return pl.BlockSpec(
            (piece, wide_here), lambda step, core_ref: (jnp.maximum(step - 2, 0), 0)
        )

    wholes = [whole((length, columns))] * rows
    return pl.pallas_call(
        kernel,
        grid_spec=pltpu.PrefetchScalarGridSpec(
            num_scalar_prefetch=1,
            grid=(4,),
            in_specs=([first_half(length)] * rows + [second_half(length)] * rows) * 2
            + wholes * 2
            + wholes
            + [second_half(lanes(length))] * rows
            + [whole(late[0][0].shape)] * rows
            + wholes,
            out_specs=pl.BlockSpec((piece, columns), lambda step, core_ref: (step, 0)),
        ),
        out_shape=jax.ShapeDtypeStruct((2 * wide, columns), jnp.float32),
        compiler_params=limit(56),
        cost_estimate=estimate(0.02),
    )(
        core.reshape(1), *dq, *dk, *dv, *attended, *normed, *branch_grad,
        *[member for place in range(2) for member in [part[place] for part in early]],
        *[member for place in range(2) for member in [part[place] for part in late]],
    )


def shards(
    hidden_in,
    row_layout,
    cotangent,
    pre_gain,
    pre_shift,
    query_weight,
    query_bias,
    key_weight,
    value_weight,
    value_bias,
    out_weight,
    out_bias,
    mid_gain,
    mid_shift,
    up_weight,
    up_bias,
    down_weight,
    down_bias,
):
    rows, length, width = hidden_in.shape
    tokens = rows * length
    heads_wide = query_weight.shape[1]
    hidden = up_weight.shape[1]
    side = sides()
    core = side["core"]
    order = Order()
    query_turned = query_weight.T
    key_turned = key_weight.T
    value_turned = value_weight.T
    up_turned = up_weight.T

    forward = [
        order.run(
            lambda ready: attention_forward(
                row, row_layout, ready, pre_gain, pre_shift, query_turned, query_bias, key_turned,
                value_turned, value_bias, out_weight,
            ),
            hidden_in,
        )
        for row in range(rows)
    ]

    up_column = up_bias.reshape(-1, 1)
    middle = []
    early = []
    for row in range(rows):
        if row > 0:
            with jax.named_scope("early_core_move_" + str(row - 1)):
                early.append(order.settle([swap(forward[row - 1].value[n], "core") for n in (6, 7)]))
        with jax.named_scope("branch_move_" + str(row)):
            received = swap_tensor(forward[row].value[5])
        middle.append(
            order.run(
                lambda ready: feed_forward(
                    row, core, hidden_in, ready, received, out_bias, mid_gain, mid_shift,
                    up_turned, up_column, down_weight, cotangent,
                    None if row == 0 else middle[row - 1].value[3],
                ),
                forward[row].value[5],
            )
        )
    with jax.named_scope("early_core_move_" + str(rows - 1)):
        early.append(order.settle([swap(forward[rows - 1].value[n], "core") for n in (6, 7)]))
    normed = [forward[row].value[0] for row in range(rows)]
    attended = [forward[row].value[4] for row in range(rows)]
    resid = [middle[row].value[0] for row in range(rows)]
    middles = [middle[row].value[1] for row in range(rows)]
    backward = []

    def back(row, received):
        _, q, k, v = forward[row].value[:4]
        backward.append(
            order.run(
                lambda ready: attention_backward(
                    row, core, row_layout, ready, received, resid[row], cotangent, mid_gain,
                    q, k, v, out_weight,
                ),
                middle[rows - 1].value[3],
            )
        )

    pairs = [middle[row].value[2] for row in range(rows)]
    ff_rows = (576, 576, 576, 576)
    ff_streams = [Stream("ff" + str(n), order, ORDERS[n], side) for n in range(4)]

    def ff_step(extra=None):
        moved = [stream.moved() for stream in ff_streams]
        received = lax.optimization_barrier(moved + ([] if extra is None else [extra]))
        for stream, part in zip(ff_streams, received):
            stream.step(part)
        return received[-1]

    lefts, rights = [], []

    def ff_core_move(row):
        with jax.named_scope("ff_core_move_" + str(row)):
            lefts.append(swap(middle[row].value[5], "core"))
            rights.append(swap(middle[row].value[6], "core"))

    ff_core_move(0)
    lefts[0] = order.settle(lefts[0])
    rights[0] = order.settle(rights[0])
    ff_core_move(1)
    ff_sides = jnp.stack([side[stream.pairs[0]] for stream in ff_streams])

    halves = order.run(
        lambda ready: ff_own(
            core, ff_sides, [pairs[0], ready], cotangent, middles, lefts, rights, ff_rows, 0
        ),
        pairs[1],
    )
    for n, stream in enumerate(ff_streams):
        stream.begin(*halves.value[2 * n : 2 * n + 2])
    with jax.named_scope("mid_move"):
        mid_received = swap_tensor(middle[rows - 1].value[3])
    back(0, mid_received)
    back(1, mid_received)

    dq, dk, dv = ([backward[row].value[place] for row in range(rows)] for place in (3, 4, 5))
    branch_grad = [backward[row].value[1] for row in range(rows)]
    output = []

    def output_move(row):
        with jax.named_scope("output_move_" + str(row)):
            return swap_tensor(middle[row].value[4])

    def output_row(row, received):
        output.append(
            order.run(
                lambda ready: low(resid[row] + (ready + received) + down_bias),
                middle[row].value[4],
            )
        )

    def normed_move(row):
        with jax.named_scope("normed_move_" + str(row)):
            return swap_tensor(normed_part[row].value)

    output_received = ff_step(output_move(0))
    late = []
    for row in range(rows):
        with jax.named_scope("late_core_move_" + str(row)):
            late.append(order.settle([swap(backward[row].value[n], "core") for n in (6, 7)]))
    at_own = order.run(
        lambda ready: attention_own(
            core, [dq[0], ready], dk, dv, attended, normed, branch_grad, early, late
        ),
        dq[1],
    )
    with jax.named_scope("at_scatter"):
        at_block = lax.psum_scatter(
            at_own.value, "dp", axis_index_groups=PLANES, scatter_dimension=0, tiled=True
        )
    normed_part = [
        order.run(
            lambda ready: inner_rows(ready, query_turned)
            + inner_rows(dk[row], key_turned)
            + inner_rows(dv[row], value_turned),
            dq[row],
        )
        for row in range(rows)
    ]
    ff_step()
    output_row(0, output_received)
    normed_received = [ff_step(normed_move(0))]
    normed_received.append(ff_step(normed_move(1)))
    normed_grad = order.run(
        lambda ready: jnp.concatenate(
            [ready + normed_received[0], normed_part[1].value + normed_received[1]], 0
        ),
        normed_part[0].value,
    )
    normed_grad.value, sum_dq, sum_dv, sum_pairs, sum_cotangent = lax.optimization_barrier(
        (normed_grad.value, dq, dv, pairs, cotangent)
    )

    pre_normal, pre_factor = normalized(hidden_in.reshape(tokens, width).astype(jnp.float32))
    pre_gain_grad = jnp.sum(normed_grad.value * pre_normal, axis=0)
    pre_shift_grad = jnp.sum(normed_grad.value, axis=0)
    resid_grad = jnp.concatenate([backward[row].value[0] for row in range(rows)], 0)
    input_grad = resid_grad + norm_back(normed_grad.value, pre_normal, pre_factor, pre_gain)
    terms = sum(backward[row].value[2] for row in range(rows))

    def token_sum(members):
        return sum(jnp.sum(member.astype(jnp.float32), axis=1) for member in members)

    small = jnp.concatenate(
        [
            pre_gain_grad,
            pre_shift_grad,
            terms[2],
            terms[0],
            terms[1],
            jnp.sum(sum_cotangent.astype(jnp.float32), axis=(0, 1)),
            token_sum(sum_dq),
            token_sum(sum_dv),
            token_sum([pair[1, :hidden] for pair in sum_pairs]),
            jnp.zeros((2 * width - hidden,), jnp.float32),
        ]
    ).reshape(9, width)
    small = order.run(lambda ready: ready, small)

    def small_move(pair):
        with jax.named_scope("small_move_" + pair):
            return swap(small.value, pair)

    def small_add(received):
        return order.run(lambda ready: ready + received, small.value)

    small = small_add(ff_step(small_move("z")))
    small = small_add(ff_step(small_move("xa")))
    small = small_add(ff_step(small_move("ya")))
    at_block = order.run(lambda ready: ready + 0.0, at_block)
    with jax.named_scope("at_z_move"):
        received = swap(at_block.value, "z")
    received = ff_step(received)
    halves = [stream.halves() for stream in ff_streams]
    at_block = order.run(lambda ready: ready + received, at_block.value)
    with jax.named_scope("at_gather"):
        at_whole = lax.all_gather(
            at_block.value, "dp", axis_index_groups=PLANES, axis=0, tiled=True
        )
    others = order.settle([other for _, other in halves] + [output_move(1)])
    output_row(1, others.pop())
    far = []
    for number, other in enumerate(others):
        with jax.named_scope("ff_core_other_" + str(number)):
            far.append((swap(halves[number][0], "core"), swap(other, "core")))
    down_up = None
    for n in range(4):
        down_up = pick_halves(
            core, ff_sides[n : n + 1], (halves[n][0], others[n], *far[n]), hidden,
            sum(ff_rows[:n]), down_up,
        )
        first_down, small.value = lax.optimization_barrier((down_up[0], small.value))
        down_up = (first_down, down_up[1])
        if n < 3:
            small = small_add(small_move(("xb", "yb", "core")[n]))
    down_grad, up_grad = down_up
    input_low, small.value, at_whole, down_grad = lax.optimization_barrier(
        (low(input_grad), small.value, at_whole, down_grad)
    )
    at_parts = [at_whole[:heads_wide], at_whole[heads_wide:]]
    at_others = []
    for number, part in enumerate(at_parts):
        with jax.named_scope("at_core_back_" + str(number)):
            at_others.append(swap(part, "core"))
    query_weight_grad, value_weight_grad = pick_rows(
        core, at_parts[0], at_others[0], heads_wide, 192, 0, 0, heads_wide
    )
    key_weight_grad, out_grad = pick_rows(
        core, at_parts[1], at_others[1], heads_wide, 192, 0, 0, heads_wide
    )
    small = small.value
    return (
        jnp.stack([part.value for part in output]),
        input_low.reshape(hidden_in.shape),
        small[0],
        small[1],
        query_weight_grad.T,
        small[6, :heads_wide],
        key_weight_grad.T,
        value_weight_grad.T,
        small[6, heads_wide:],
        out_grad,
        small[2],
        small[3],
        small[4],
        up_grad.T,
        small[7:].reshape(-1)[:hidden],
        down_grad,
        small[5],
    )


def solution(mesh):
    placed = (
        P("dp", None, None),
        P("dp", None),
        P("dp", None, None),
        P(),
        P(),
        P(None, "tensor"),
        P("tensor"),
        P(None, "tensor"),
        P(None, "tensor"),
        P("tensor"),
        P("tensor", None),
        P(),
        P(),
        P(),
        P(None, "tensor"),
        P("tensor"),
        P("tensor", None),
        P(),
    )
    return jax.shard_map(
        shards,
        mesh=mesh,
        in_specs=placed,
        out_specs=(
            P("dp", None, None),
            P("dp", None, None),
            P(),
            P(),
            P(None, "tensor"),
            P("tensor"),
            P(None, "tensor"),
            P(None, "tensor"),
            P("tensor"),
            P("tensor", None),
            P(),
            P(),
            P(),
            P(None, "tensor"),
            P("tensor"),
            P("tensor", None),
            P(),
        ),
        check_vma=False,
    )
```
